1024 devices in a mesh: dp: 16 (over y, core), table: 64 (over x, z).
Axes of the slice: x: 4, y: 8, z: 16, core: 2. Of those that a mesh axis runs over, the one named last changes fastest.
Arguments:
- table: float32 [131072, 256], P(('dp', 'table')), may hold values from -6 to 6
- accum: float32 [131072], P(('dp', 'table')), may hold values from 0.05 to 2
- item_weight: bfloat16 [256, 256], replicated, may hold values from -0.375 to 0.375
- query_weight: bfloat16 [256, 256], replicated, may hold values from -0.375 to 0.375
- packed_rows: int32 [16, 64, 1536], P('dp', 'table'), may hold values from 0 to 127
- block_counts: int32 [16, 64, 1024], P('dp', 'table'), may hold values from 1 to 2, 1536 in all within a row
- item_refs: int32 [16, 64, 128, 4], P('dp', 'table'), may hold values from 0 to 1535
- query_refs: int32 [16, 64, 128, 4], P('dp', 'table'), may hold values from 0 to 1535
Outputs:
- new_table: float32 [131072, 256], P(('dp', 'table'))
- new_accum: float32 [131072], P(('dp', 'table'))
- pair_loss: float32 [16, 64, 128], P('dp', 'table')
The draws below stay inside these ranges and needn't reach their ends.
Inputs may be any that keep to these rules, and one draw needn't show every extreme that they name: `block_counts`: each device's 1024 counts sum to 1536, every count is at least 1, and in every device's list some owner gets exactly 2 entries. `packed_rows`: a row number within the shard of the owner that its position belongs to; rows may repeat. `item_refs`: positions in the same device's packed list; they repeat. `query_refs`: positions in the same device's packed list; they repeat.
All inputs are finite; a program needn't handle non-finite values.
Results may differ from the reference program's by a relative error of at most 0.0026.
Values may be sent and summed in bfloat16 or wider, within the bound.
No kernel may reach another device: no remote copies, remote signals or barrier semaphores. Data moves between devices by JAX's collectives and lax.ppermute only.
A program may use at most 32 MiB of HBM per device.

```python
import math
import jax
import jax.numpy as jnp
import numpy as np
from jax import lax

D = 256
PAIR_DEV = 128
ROWS_DEV = 128
CAP = 2
ITEM_LEN = 4
QUERY_LEN = 4
R_DEV = 1536
ROWS = 131072
N_DP = 16
N_TABLE = 64
DEVICES = 1024


def set_ends(entries, stream_key, low, top_value):
    shape = entries.shape
    spot = [jax.random.randint(jax.random.fold_in(stream_key, axis), (), 0, shape[axis]) for axis in range(len(shape))]
    entries = entries.at[tuple(spot)].set(low)
    longest = shape.index(max(shape))
    spot[longest] = (spot[longest] + 1) % shape[longest]
    return entries.at[tuple(spot)].set(top_value)


def level_of(own_key, extent, pieces, least, top_value):
    def one(axis_at, parts):
        heights = jax.random.uniform(jax.random.fold_in(jax.random.fold_in(own_key, 6), axis_at), (parts,), jnp.float32, least / len(pieces), top_value / len(pieces))
        return jnp.repeat(jnp.exp(heights), extent[axis_at] // parts).reshape((-1,) + (1,) * (len(extent) - axis_at - 1))

    loudness = one(*pieces[0])
    for cut in pieces[1:]:
        loudness = loudness * one(*cut)
    return loudness


def rank_table(number_of, lean):
    weights = [(1 << 20) // math.isqrt(standing ** lean) + 1 for standing in range(1, number_of + 1)]
    scale = 1 + sum(weights) // (1 << 30)
    return np.cumsum(np.array([max(1, weight // scale) for weight in weights]))


def ranked_ids(own_key, dims, count, skew):
    listing = rank_table(count, skew)
    ticket = jax.random.randint(jax.random.fold_in(own_key, 1), dims, 0, int(listing[count - 1]))
    standing = jnp.searchsorted(jnp.asarray(listing, jnp.int32), ticket, side="right")
    return jax.random.permutation(jax.random.fold_in(own_key, 2), count)[standing].astype(jnp.int32)


def length_profile(amount, total, reach, slope):
    weights = [(1 << 20) // math.isqrt(grade ** slope) + 1 for grade in range(2, amount + 1)]
    surplus, given = total - reach - (amount - 1), [1] * (amount - 1)
    while surplus > 0:
        candidates = [i for i in range(amount - 1) if given[i] < reach]
        mass, remaining = sum([weights[i] for i in candidates]), surplus
        for i in candidates:
            extra = min(reach - given[i], max(1, remaining * weights[i] // mass), surplus)
            given[i] = given[i] + extra
            surplus = surplus - extra
    return np.array([reach] + given)


def ragged_sizes(stream_key, number_of, total, limit, skew):
    if number_of == 2:
        one = jax.random.randint(stream_key, (), max(1, total - limit), min(limit, total - 1) + 1)
        return jnp.stack([one, total - one])
    tallies = jnp.asarray(length_profile(number_of, total, limit, skew), jnp.int32)
    pairs = (number_of - 1) // 2
    source_of, sink = tallies[1:1 + 2 * pairs:2], tallies[2:2 + 2 * pairs:2]
    slack = jnp.minimum(source_of - 1, limit - sink)
    passed = jax.random.randint(jax.random.fold_in(stream_key, 1), (pairs,), 0, 1 << 20) % (slack + 1)
    tallies = tallies.at[1:1 + 2 * pairs:2].set(source_of - passed).at[2:2 + 2 * pairs:2].set(sink + passed)
    return tallies[jax.random.permutation(jax.random.fold_in(stream_key, 2), number_of)]


def centred(stream_key, dims, scale, limit, pieces=(), kind=jnp.bfloat16):
    factor_of = level_of(stream_key, dims, pieces, -0.22, 0.18) if pieces else 1.0
    drawn = jax.random.normal(stream_key, dims, jnp.float32) * scale * factor_of
    return jnp.minimum(jnp.maximum(drawn, -limit), limit).astype(kind)


def setup_inputs(seed: int = 0) -> dict:
    seeds = jax.random.split(jax.random.key(seed), 9)
    table = centred(seeds[0], (ROWS, D), 1.0, 6.0, ((0, 1024),), jnp.float32)
    accum = jnp.clip(jnp.exp(math.log(2.0) - 3.6888794 * jax.random.uniform(seeds[1], (ROWS,), jnp.float32) ** level_of(seeds[1], (ROWS,), ((0, 1024),), -0.2, 0.2)), 0.05, 2.0)
    item_weight = centred(seeds[2], (D, D), D ** -0.5, 0.375)
    query_weight = centred(seeds[3], (D, D), D ** -0.5, 0.375)
    packed_rows = set_ends(ranked_ids(seeds[4], (N_DP, N_TABLE, R_DEV), ROWS_DEV, 2), jax.random.fold_in(seeds[4], 3), 0, ROWS_DEV - 1).astype(jnp.int32)
    block_counts = jax.vmap(lambda own: ragged_sizes(own, DEVICES, R_DEV, CAP, 2))(jax.random.split(seeds[5], N_DP * N_TABLE)).reshape((N_DP, N_TABLE, DEVICES)).astype(jnp.int32)
    item_refs = set_ends(ranked_ids(seeds[6], (N_DP, N_TABLE, PAIR_DEV, ITEM_LEN), R_DEV, 2), jax.random.fold_in(seeds[6], 3), 0, R_DEV - 1).astype(jnp.int32)
    query_refs = set_ends(ranked_ids(seeds[7], (N_DP, N_TABLE, PAIR_DEV, QUERY_LEN), R_DEV, 1), jax.random.fold_in(seeds[7], 3), 0, R_DEV - 1).astype(jnp.int32)
    return {"table": table, "accum": accum, "item_weight": item_weight, "query_weight": query_weight, "packed_rows": packed_rows, "block_counts": block_counts, "item_refs": item_refs, "query_refs": query_refs}


learn_rate = 0.3
epsilon = 1e-06
sharpness = 3.0

def project(pooled, weight):
    hidden = jnp.dot(pooled, weight, preferred_element_type=jnp.float32)
    factor = lax.rsqrt(lax.optimization_barrier(jnp.mean(hidden * hidden, axis=1, keepdims=True)) + epsilon)
    return (hidden * factor, factor)

def project_back(grad_out, normed, factor, weight):
    inner_mean = lax.optimization_barrier(jnp.mean(grad_out * normed, axis=1, keepdims=True))
    grad_hidden = (factor * (grad_out - normed * inner_mean)).astype(jnp.bfloat16)
    return lax.dot_general(grad_hidden, weight, (((1,), (1,)), ((), ())), preferred_element_type=jnp.float32)

def reference(table, accum, item_weight, query_weight, packed_rows, block_counts, item_refs, query_refs):
    replica_count = packed_rows.shape[0]
    owner_count = packed_rows.shape[1]
    list_length = packed_rows.shape[2]
    pair_count = item_refs.shape[2]
    feature_width = table.shape[1]
    score_scale = sharpness * feature_width ** (-0.5)
    block_ends = jnp.cumsum(block_counts, axis=-1).astype(jnp.int32)
    positions = jnp.arange(list_length, dtype=jnp.int32)

    def find_owner(ends):
        return jnp.searchsorted(ends, positions, side='right').astype(jnp.int32)
    flat_ends = block_ends.reshape(-1, block_counts.shape[-1])
    owners = jax.vmap(find_owner)(flat_ends).astype(jnp.int32).reshape(packed_rows.shape)
    global_ids = (owners * ROWS_DEV + packed_rows).astype(jnp.int32)
    item_ids = jnp.take_along_axis(global_ids, item_refs.reshape(replica_count, owner_count, -1), axis=2)
    item_ids = jnp.transpose(item_ids.reshape(item_refs.shape), (1, 0, 2, 3))
    query_ids = jnp.take_along_axis(global_ids, query_refs.reshape(replica_count, owner_count, -1), axis=2)
    query_ids = jnp.transpose(query_ids.reshape(query_refs.shape), (1, 0, 2, 3))
    rows_bf = table.astype(jnp.bfloat16)
    group_size = replica_count * pair_count
    diagonal = jnp.eye(group_size, dtype=jnp.float32)

    def pool_rows(row_ids):
        summed = lax.optimization_barrier(jnp.sum(rows_bf[row_ids].astype(jnp.float32), axis=-2))
        return summed.reshape(group_size, feature_width).astype(jnp.bfloat16)

    def spread(row_grads, row_ids, back):
        depth = row_ids.shape[-1]
        widened = jnp.broadcast_to(back.reshape(replica_count, pair_count, 1, feature_width), (replica_count, pair_count, depth, feature_width))
        return row_grads.at[row_ids.reshape(-1)].add(widened.reshape(-1, feature_width))

    def group_step(row_grads, id_lists):
        item_group, query_group = id_lists
        item_normed, item_factor = project(pool_rows(item_group), item_weight)
        query_normed, query_factor = project(pool_rows(query_group), query_weight)
        item_out = item_normed.astype(jnp.bfloat16)
        query_out = query_normed.astype(jnp.bfloat16)
        scores = lax.dot_general(query_out, item_out, (((1,), (1,)), ((), ())), preferred_element_type=jnp.float32) * score_scale
        totals = jnp.log(lax.optimization_barrier(jnp.sum(jnp.exp(scores), axis=1)))
        losses = totals - lax.optimization_barrier(jnp.sum(scores * diagonal, axis=1))
        grad_scores = (jnp.exp(scores - totals[:, None]) - diagonal).astype(jnp.bfloat16)
        grad_query = jnp.dot(grad_scores, item_out, preferred_element_type=jnp.float32) * score_scale
        grad_item = lax.dot_general(grad_scores, query_out, (((0,), (0,)), ((), ())), preferred_element_type=jnp.float32) * score_scale
        item_back = project_back(grad_item, item_normed, item_factor, item_weight)
        query_back = project_back(grad_query, query_normed, query_factor, query_weight)
        row_grads = spread(row_grads, item_group, item_back)
        row_grads = spread(row_grads, query_group, query_back)
        return (row_grads, losses.reshape(replica_count, pair_count))
    row_grads, losses = lax.scan(group_step, jnp.zeros(table.shape, jnp.float32), (item_ids, query_ids))
    new_accum = accum + lax.optimization_barrier(jnp.mean(row_grads * row_grads, axis=1))
    new_table = table - learn_rate * row_grads / jnp.sqrt(new_accum)[:, None]
    pair_loss = jnp.transpose(losses, (1, 0, 2))
    return (new_table, new_accum, pair_loss)
```

```python
import jax
import jax.numpy as jnp
from jax import lax
from jax.experimental import pallas as pl
from jax.experimental.pallas import tpu as pltpu
from jax.sharding import PartitionSpec as P

CAP = 2
LANES = 128
CORES = 2

learn_rate = 0.3
epsilon = 1e-06
sharpness = 3.0

VMEM = pl.BlockSpec(memory_space=pltpu.VMEM)
SMEM = pl.BlockSpec(memory_space=pltpu.SMEM)

NT = (((1,), (1,)), ((), ()))
TN = (((0,), (0,)), ((), ()))


def iota(shape, axis):
    return lax.broadcasted_iota(jnp.int32, shape, axis)


def dot(a, b, dims=(((1,), (0,)), ((), ()))):
    return lax.dot_general(a, b, dims, preferred_element_type=jnp.float32)


def hits(a, b):
    return jnp.where(a == b, 1.0, 0.0)


def call(body, out_shape, in_specs, scratch=()):
    return pl.pallas_call(
        body,
        out_shape=out_shape,
        in_specs=in_specs,
        out_specs=jax.tree.map(lambda _: VMEM, out_shape),
        scratch_shapes=list(scratch),
        compiler_params=pltpu.CompilerParams(vmem_limit_bytes=40 * 1024 * 1024),
    )


def request_body(core_ref, list_ref, counts_ref, req_ref, pos_ref, list2d, counts2d, square):
    length, owners = list_ref.shape[1], counts_ref.shape[1]
    list2d[...] = jnp.zeros_like(list2d)
    for b in range(length // LANES):
        list2d[b : b + 1, :] = list_ref[:, b * LANES : (b + 1) * LANES].astype(jnp.float32)
    for b in range(owners // LANES):
        counts2d[b : b + 1, :] = counts_ref[:, b * LANES : (b + 1) * LANES].astype(jnp.float32)
    rows = owners // LANES
    counts = counts2d[...]
    counts_bf = counts.astype(jnp.bfloat16)
    before = hits(iota((LANES, LANES), 0) < iota((LANES, LANES), 1), True).astype(jnp.bfloat16)
    within = dot(counts_bf, before)
    row_total = dot(counts_bf, jnp.ones((LANES, LANES), jnp.bfloat16))
    base = [jnp.zeros((1, LANES), jnp.float32)]
    for i in range(rows - 1):
        base.append(base[-1] + row_total[i : i + 1, :])
    starts = within + jnp.concatenate(base, axis=0)
    second = jnp.where(counts > 1.5, starts + 1.0, -1.0)
    positions = jnp.concatenate([starts, second], axis=0)
    pos_int = positions.astype(jnp.int32)
    list_bf = list2d[...].astype(jnp.bfloat16)
    down = iota((LANES, LANES), 0)
    block = iota((list2d.shape[0], LANES), 0)
    picked = []
    for r in range(CAP * rows):
        p = pos_int[r : r + 1, :]
        spread = dot(list_bf, hits(down, p & (LANES - 1)).astype(jnp.bfloat16))
        value = jnp.sum(jnp.where(block == (p >> 7), spread, 0.0), axis=0, keepdims=True)
        picked.append(jnp.where(p >= 0, value, -1.0))
    width = LANES // CORES
    mine = core_ref[0] == 0
    for out_ref, values in ((req_ref, jnp.concatenate(picked, axis=0)), (pos_ref, positions)):
        square[...] = jnp.zeros_like(square)
        square[0 : CAP * rows, :] = values
        turned = square[...].T
        first, other = turned[:width, : CAP * rows], turned[width:, : CAP * rows]
        swapped = jnp.concatenate(
            [jnp.where(mine, first, other), jnp.where(mine, other, first)], axis=1
        )
        out_ref[...] = swapped.astype(jnp.int32)


def pick_body(recv_ref, near_ref, far_ref, out_ref, *wide):
    groups, slots = recv_ref.shape
    chips, per = near_ref.shape[:2]
    recv = recv_ref[...]
    lane = iota((groups, per), 1)
    for side, rows_ref in enumerate((near_ref, far_ref)):
        for y in range(chips):
            ks = [side * CAP * chips + c * chips + y for c in range(CAP)]
            wanted = jnp.concatenate([hits(lane, recv[:, k : k + 1]) for k in ks], axis=0)
            got = dot(wanted.astype(jnp.bfloat16), rows_ref[y])
            for c, k in enumerate(ks):
                for b, half in enumerate(wide):
                    half[pl.ds(k, groups, stride=slots), :] = got[
                        c * groups : (c + 1) * groups, b * LANES : (b + 1) * LANES
                    ]
    for b, half in enumerate(wide):
        out_ref[:, b * LANES : (b + 1) * LANES] = half[...].astype(jnp.bfloat16)


def tower_body(
    pos_ref, item_refs, query_refs, fetched, item_w, query_w, hits_ref, normed_ref, factor_ref, out_ref
):
    pairs = item_refs.shape[0]
    fetched_rows = fetched[...]
    pos = pos_ref[...]
    outs = []
    for side, (refs_ref, w_ref) in enumerate(((item_refs, item_w), (query_refs, query_w))):
        span = pl.ds(side * pairs, pairs)
        refs = refs_ref[...]
        weight = hits(refs[:, 0:1], pos)
        for l in range(1, refs.shape[1]):
            weight = weight + hits(refs[:, l : l + 1], pos)
        weight = weight.astype(jnp.bfloat16)
        hits_ref[span, :] = weight
        pool = dot(weight, fetched_rows).astype(jnp.bfloat16)
        hidden = dot(pool, w_ref[...])
        factor = lax.rsqrt(jnp.mean(hidden * hidden, axis=1, keepdims=True) + epsilon)
        normed = hidden * factor
        normed_ref[span, :] = normed
        factor_ref[span, :] = jnp.broadcast_to(factor, (pairs, LANES))
        outs.append(normed.astype(jnp.bfloat16))
    for y in range(out_ref.shape[0]):
        out_ref[y, :pairs, :] = outs[0]
        out_ref[y, pairs:, :] = outs[1]


def loss_body(
    y_ref, near, far, normed_ref, factor_ref, item_w, query_w, hits_ref, loss_ref, grads_ref, inverse, own_exp
):
    chips, both, width = near.shape
    pairs = both // 2
    scale = sharpness * width ** (-0.5)
    own = y_ref[0]

    def items(y):
        return jnp.concatenate([near[y, :pairs, :], far[y, :pairs, :]], axis=0)

    def queries(y):
        return jnp.concatenate([near[y, pairs:, :], far[y, pairs:, :]], axis=0)

    def denominators(y, carry):
        q = queries(y)
        total = jnp.zeros((8, both), jnp.float32)
        for j in range(chips):
            e = jnp.exp(dot(items(j), q, NT) * scale)
            total = total + jnp.sum(e.reshape(both // 8, 8, both), axis=0)
        inverse[y] = jnp.sum(total, axis=0, keepdims=True)
        return carry

    lax.fori_loop(0, chips, denominators, 0)
    item_own, query_own = near[own, :pairs, :], near[own, pairs:, :]
    own_hits = iota((pairs, pairs), 0) == iota((pairs, pairs), 1)
    diagonal = jnp.sum(
        jnp.where(own_hits, dot(item_own, query_own, NT) * scale, 0.0), axis=0, keepdims=True
    )
    loss_ref[...] = jnp.log(inverse[own][:, :pairs]) - diagonal
    ones = hits(iota((pairs, both), 0), iota((pairs, both), 1))
    grad_item = jnp.zeros((pairs, width), jnp.float32)
    row_total = jnp.zeros((pairs, LANES), jnp.float32)
    for y in range(chips):
        q = queries(y)
        soft = jnp.exp(dot(item_own, q, NT) * scale) * (1.0 / inverse[y])
        soft = soft - jnp.where(own == y, ones, 0.0)
        grad_item = grad_item + dot(soft.astype(jnp.bfloat16), q)
        e = jnp.exp(dot(query_own, items(y), NT) * scale)
        own_exp[y] = e
        for b in range(both // LANES):
            row_total = row_total + e[:, b * LANES : (b + 1) * LANES]
    row_inverse = 1.0 / jnp.sum(row_total, axis=1, keepdims=True)
    grad_query = jnp.zeros((pairs, width), jnp.float32)
    for y in range(chips):
        soft = own_exp[y] * row_inverse - jnp.where(own == y, ones, 0.0)
        grad_query = grad_query + dot(soft.astype(jnp.bfloat16), items(y))
    backs = []
    for side, (grad, w_ref) in enumerate(((grad_item, item_w), (grad_query, query_w))):
        span = pl.ds(side * pairs, pairs)
        grad = grad * scale
        normed = normed_ref[span, :]
        factor = factor_ref[span, 0:1]
        inner_mean = jnp.mean(grad * normed, axis=1, keepdims=True)
        grad_hidden = (factor * (grad - normed * inner_mean)).astype(jnp.bfloat16)
        backs.append(dot(grad_hidden, w_ref[...], NT))
    back = jnp.concatenate(backs, axis=0)
    high = back.astype(jnp.bfloat16)
    low = (back - high.astype(jnp.float32)).astype(jnp.bfloat16)
    step = 256
    for s in range(hits_ref.shape[1] // step):
        weight = hits_ref[:, s * step : (s + 1) * step]
        grads_ref[s * step : (s + 1) * step, :] = (
            dot(weight, high, TN) + dot(weight, low, TN)
        ).astype(jnp.bfloat16)


def column_body(recv_ref, grads_ref, keep_ref, send_ref, square, *wide):
    groups, slots = recv_ref.shape
    chips = slots // (CAP * CORES)
    per = keep_ref.shape[1]
    square[...] = jnp.full_like(square, -1.0)
    square[0:groups, 0:slots] = recv_ref[...].astype(jnp.float32)
    turned = square[...].T.astype(jnp.int32)
    for b, half in enumerate(wide):
        half[...] = grads_ref[:, b * LANES : (b + 1) * LANES].astype(jnp.float32)
    down = iota((per, CAP * groups), 0)
    for side in (1, 0):
        for y in range(chips):
            ks = [side * CAP * chips + c * chips + y for c in range(CAP)]
            wanted = jnp.concatenate([turned[k : k + 1, :groups] for k in ks], axis=1)
            values = jnp.concatenate(
                [
                    jnp.concatenate([half[pl.ds(k, groups, stride=slots), :] for half in wide], axis=1)
                    for k in ks
                ],
                axis=0,
            ).astype(jnp.bfloat16)
            summed = dot(hits(down, wanted).astype(jnp.bfloat16), values)
            if side == 1:
                send_ref[y] = summed.astype(jnp.bfloat16)
            else:
                keep_ref[y] = summed


def add_body(a_ref, b_ref, out_ref):
    out_ref[...] = (a_ref[...] + b_ref[...].astype(jnp.float32)).astype(jnp.bfloat16)


def adagrad_body(parts_ref, table_ref, accum_ref, new_table_ref, new_accum_ref):
    grad = parts_ref[0].astype(jnp.float32)
    for y in range(1, parts_ref.shape[0]):
        grad = grad + parts_ref[y].astype(jnp.float32)
    rows, width = grad.shape
    mean = jnp.sum(grad * grad, axis=1, keepdims=True) * (1.0 / width)
    across = jnp.sum(
        jnp.where(iota((rows, rows), 0) == iota((rows, rows), 1), mean, 0.0), axis=0, keepdims=True
    )
    down = jnp.sum(
        jnp.where(iota((rows, rows), 0) == iota((rows, rows), 1), accum_ref[...], 0.0),
        axis=1,
        keepdims=True,
    )
    new_accum_ref[...] = accum_ref[...] + across
    new_table_ref[...] = table_ref[...] - learn_rate * grad / jnp.sqrt(down + mean)


def on_device(
    table, accum, item_weight, query_weight, packed_rows, block_counts, item_refs, query_refs
):
    bf16, f32, i32 = jnp.bfloat16, jnp.float32, jnp.int32
    shape = jax.ShapeDtypeStruct
    n_dp, n_table = lax.axis_size("dp"), lax.axis_size("table")
    chips = n_dp // CORES
    per, width = table.shape
    pairs = item_refs.shape[2]
    slots = CAP * n_dp
    total = slots * n_table
    replica = lax.axis_index("dp")
    core = (replica % CORES).reshape(1).astype(i32)
    chip = (replica // CORES).reshape(1).astype(i32)
    along_y = [[y * CORES + c for y in range(chips)] for c in range(CORES)]
    swap = [(r, r ^ 1) for r in range(n_dp)]

    near_rows = lax.all_to_all(
        jnp.broadcast_to(table.astype(bf16)[None], (chips, per, width)),
        "dp",
        split_axis=0,
        concat_axis=0,
        axis_index_groups=along_y,
        tiled=True,
    )
    far_rows = lax.ppermute(near_rows, "dp", swap)
    requests, positions = call(
        request_body,
        (shape((n_table, slots), i32), shape((n_table, slots), i32)),
        [SMEM, VMEM, VMEM],
        [
            pltpu.VMEM((16, LANES), f32),
            pltpu.VMEM((n_dp * n_table // LANES, LANES), f32),
            pltpu.VMEM((LANES, LANES), f32),
        ],
    )(core, packed_rows.reshape(1, -1), block_counts.reshape(1, -1))
    received = lax.all_to_all(requests, "table", split_axis=0, concat_axis=0, tiled=True)
    picked = call(
        pick_body,
        shape((total, width), bf16),
        [VMEM] * 3,
        [pltpu.VMEM((total, LANES), f32)] * (width // LANES),
    )(received, near_rows, far_rows)
    fetched = lax.all_to_all(
        picked.reshape(n_table, slots, width), "table", split_axis=0, concat_axis=0, tiled=True
    ).reshape(total, width)
    pair_hits, normed, factor, spread = call(
        tower_body,
        (
            shape((2 * pairs, total), bf16),
            shape((2 * pairs, width), f32),
            shape((2 * pairs, LANES), f32),
            shape((chips, 2 * pairs, width), bf16),
        ),
        [VMEM] * 6,
    )(positions.reshape(1, total), item_refs[0, 0], query_refs[0, 0], fetched, item_weight, query_weight)
    near = lax.all_to_all(
        spread, "dp", split_axis=0, concat_axis=0, axis_index_groups=along_y, tiled=True
    )
    far = lax.ppermute(near, "dp", swap)
    loss, slot_grads = call(
        loss_body,
        (shape((1, pairs), f32), shape((total, width), bf16)),
        [SMEM] + [VMEM] * 7,
        [pltpu.VMEM((chips, 1, 2 * pairs), f32), pltpu.VMEM((chips, pairs, 2 * pairs), f32)],
    )(chip, near, far, normed, factor, item_weight, query_weight, pair_hits)
    returned = lax.all_to_all(
        slot_grads.reshape(n_table, slots, width), "table", split_axis=0, concat_axis=0, tiled=True
    ).reshape(total, width)
    keep, send = call(
        column_body,
        (shape((chips, per, width), f32), shape((chips, per, width), bf16)),
        [VMEM] * 2,
        [pltpu.VMEM((LANES, LANES), f32)] + [pltpu.VMEM((total, LANES), f32)] * (width // LANES),
    )(received, returned)
    other = lax.ppermute(send, "dp", swap)
    both = call(add_body, shape((chips, per, width), bf16), [VMEM] * 2)(keep, other)
    parts = lax.all_to_all(
        both, "dp", split_axis=0, concat_axis=0, axis_index_groups=along_y, tiled=True
    )
    new_table, new_accum = call(
        adagrad_body, (shape((per, width), f32), shape((1, per), f32)), [VMEM] * 3
    )(parts, table, accum.reshape(1, per))
    return (new_table, new_accum.reshape(per), loss.reshape(1, 1, pairs))


def solution(mesh):
    in_specs = (
        P(("dp", "table"), None),
        P(("dp", "table")),
        P(),
        P(),
        P("dp", "table", None),
        P("dp", "table", None),
        P("dp", "table", None, None),
        P("dp", "table", None, None),
    )
    out_specs = (P(("dp", "table"), None), P(("dp", "table")), P("dp", "table", None))
    return jax.shard_map(
        on_device, mesh=mesh, in_specs=in_specs, out_specs=out_specs, check_vma=False
    )
```

```python
import functools

import jax
import jax.numpy as jnp
from jax import lax
from jax.experimental import pallas as pl
from jax.experimental.pallas import tpu as pltpu
from jax.sharding import PartitionSpec as P

CAP = 2
LANES = 128
CORES = 2

learn_rate = 0.3
epsilon = 1e-06
sharpness = 3.0

VMEM = pl.BlockSpec(memory_space=pltpu.VMEM)
SMEM = pl.BlockSpec(memory_space=pltpu.SMEM)

NT = (((1,), (1,)), ((), ()))
TN = (((0,), (0,)), ((), ()))


def iota(shape, axis):
    return lax.broadcasted_iota(jnp.int32, shape, axis)


def dot(a, b, dims=(((1,), (0,)), ((), ()))):
    return lax.dot_general(a, b, dims, preferred_element_type=jnp.float32)


def hits(a, b):
    return jnp.where(a == b, 1.0, 0.0)


def call(body, out_shape, in_specs, scratch=(), out_specs=None):
    return pl.pallas_call(
        body,
        out_shape=out_shape,
        in_specs=in_specs,
        out_specs=jax.tree.map(lambda _: VMEM, out_shape) if out_specs is None else out_specs,
        scratch_shapes=list(scratch),
        compiler_params=pltpu.CompilerParams(vmem_limit_bytes=24 * 1024 * 1024),
    )


def request_body(
    core_ref, list_ref, counts_ref, item_refs, query_refs, req_ref, pos_ref, looked, counts2d, square, *, base
):
    length, owners = list_ref.shape[1], counts_ref.shape[1]
    rows = owners // LANES
    depth = looked.shape[0] // 2
    groups, slots = pos_ref.shape
    looked[...] = jnp.zeros_like(looked)
    for b in range(length // LANES):
        looked[b : b + 1, :] = list_ref[:, b * LANES : (b + 1) * LANES].astype(jnp.float32)
    for b in range(rows):
        counts2d[b : b + 1, :] = counts_ref[:, b * LANES : (b + 1) * LANES].astype(jnp.float32)
    down = iota((LANES, LANES), 0)
    block = iota((depth, LANES), 0)
    wanted = jnp.zeros((depth, LANES), jnp.float32)
    for refs_ref in (item_refs, query_refs):
        for l in range(refs_ref.shape[0]):
            ref = refs_ref[l : l + 1, :]
            high = hits(block, ref >> 7).astype(jnp.bfloat16)
            low = hits(down, ref & (LANES - 1)).astype(jnp.bfloat16)
            wanted = wanted + dot(high, low, NT)
    looked[depth:, :] = jnp.where(wanted > 0.5, 1.0, 0.0)
    looked_bf = looked[...].astype(jnp.bfloat16)

    counts = counts2d[...]
    counts_bf = counts.astype(jnp.bfloat16)
    before = hits(down < iota((LANES, LANES), 1), True).astype(jnp.bfloat16)
    within = dot(counts_bf, before)
    row_total = dot(counts_bf, jnp.ones((LANES, LANES), jnp.bfloat16))
    offsets = [jnp.zeros((1, LANES), jnp.float32)]
    for i in range(rows - 1):
        offsets.append(offsets[-1] + row_total[i : i + 1, :])
    starts = within + jnp.concatenate(offsets, axis=0)
    second = jnp.where(counts > 1.5, starts + 1.0, -1.0)
    positions = jnp.concatenate([starts, second], axis=0)
    pos_int = positions.astype(jnp.int32)
    entries = CAP * rows
    width = LANES // CORES
    owner_core = jnp.where(iota((1, LANES), 1) < width, 0, 1)
    side = jnp.where(owner_core == core_ref[0], 0.0, 1.0)
    square[...] = jnp.zeros_like(square)
    square[entries : 2 * entries, :] = positions
    for r in range(entries):
        p = pos_int[r : r + 1, :]
        spread = dot(looked_bf, hits(down, p & (LANES - 1)).astype(jnp.bfloat16))
        here = block == (p >> 7)
        value = jnp.sum(jnp.where(here, spread[:depth], 0.0), axis=0, keepdims=True)
        used = jnp.sum(jnp.where(here, spread[depth:], 0.0), axis=0, keepdims=True)
        square[r : r + 1, :] = value + (side * rows + (r % rows)) * LANES
        square[2 * entries + r : 2 * entries + r + 1, :] = used
    turned = square[...].T

    def column(n):
        part = slice(n * entries, (n + 1) * entries)
        return jnp.concatenate([turned[:width, part], turned[width:, part]], axis=1)

    codes, places, used = column(0), column(1), column(2)
    before = hits(iota((slots, slots), 0) < iota((slots, slots), 1), True).astype(jnp.bfloat16)
    rank = dot(used.astype(jnp.bfloat16), before)
    rank = jnp.where(used > 0.5, rank, -1.0).astype(jnp.int32)
    slot = iota((groups, slots), 1)
    packed_codes = jnp.full((groups, slots), -1.0, jnp.float32)
    packed_places = packed_codes
    for k in range(slots):
        here = slot == rank[:, k : k + 1]
        packed_codes = jnp.where(here, codes[:, k : k + 1], packed_codes)
        packed_places = jnp.where(here, places[:, k : k + 1], packed_places)
    over = jnp.max(rank, axis=1, keepdims=True)
    over = jnp.max(over, axis=0, keepdims=True)
    over = jnp.where(over >= base, 1, 0)
    pos_ref[...] = packed_places.astype(jnp.int32)
    req_ref[:, :slots] = packed_codes.astype(jnp.int32)
    req_ref[:, slots:] = jnp.broadcast_to(over, (groups, req_ref.shape[1] - slots))


def pick_body(recv_ref, near_ref, far_ref, out_ref, over_ref, square, *, first, count, slots):
    groups = recv_ref.shape[0]
    chips, per, width = near_ref.shape
    square[...] = jnp.zeros_like(square)
    square[:groups, : recv_ref.shape[1]] = recv_ref[...].astype(jnp.float32)
    turned = square[...].T.astype(jnp.int32)
    over_ref[0] = jnp.max(turned[slots : slots + 1, :groups])
    lane = iota((count, LANES), 1)
    rows = jnp.concatenate(
        [near_ref[...].reshape(chips * per, width), far_ref[...].reshape(chips * per, width)], axis=0
    )
    step = 8
    for t in range(0, groups, step):
        hot = []
        for u in range(t, t + step):
            code = jnp.broadcast_to(turned[first : first + count, u : u + 1], (count, LANES))
            hot.append(
                jnp.concatenate(
                    [hits(lane + b * LANES, code) for b in range(rows.shape[0] // LANES)], axis=1
                )
            )
        hot = jnp.concatenate(hot, axis=0).astype(jnp.bfloat16)
        out_ref[t * count : (t + step) * count, :] = dot(hot, rows).astype(jnp.bfloat16)


def pair_weight(refs, pos):
    weight = hits(refs[:, 0:1], pos)
    for l in range(1, refs.shape[1]):
        weight = weight + hits(refs[:, l : l + 1], pos)
    return weight.astype(jnp.bfloat16)


def tower_body(
    pos_ref, more_pos_ref, item_refs, query_refs, fetched, more_fetched, item_w, query_w,
    hits_ref, more_hits_ref, normed_ref, factor_ref, out_ref, square,
):
    pairs = item_refs.shape[1]
    square[...] = jnp.zeros_like(square)
    square[0 : item_refs.shape[0], :] = item_refs[...].astype(jnp.float32)
    square[8 : 8 + query_refs.shape[0], :] = query_refs[...].astype(jnp.float32)
    turned = square[...].T.astype(jnp.int32)
    item_columns = turned[:, 0 : item_refs.shape[0]]
    query_columns = turned[:, 8 : 8 + query_refs.shape[0]]
    outs = []
    for side, (refs, w_ref) in enumerate(((item_columns, item_w), (query_columns, query_w))):
        span = pl.ds(side * pairs, pairs)
        weight = pair_weight(refs, pos_ref[...])
        more_weight = pair_weight(refs, more_pos_ref[...])
        hits_ref[span, :] = weight
        more_hits_ref[span, :] = more_weight
        pool = (dot(weight, fetched[...]) + dot(more_weight, more_fetched[...])).astype(jnp.bfloat16)
        hidden = dot(pool, w_ref[...])
        factor = lax.rsqrt(jnp.mean(hidden * hidden, axis=1, keepdims=True) + epsilon)
        normed = hidden * factor
        normed_ref[span, :] = normed
        factor_ref[span, :] = jnp.broadcast_to(factor, (pairs, LANES))
        outs.append(normed.astype(jnp.bfloat16))
    for y in range(out_ref.shape[0]):
        out_ref[y, :pairs, :] = outs[0]
        out_ref[y, pairs:, :] = outs[1]


def scale_of(width):
    return sharpness * width ** (-0.5)


def near_body(near, sums_ref):
    chips, both, width = near.shape
    pairs = both // 2
    for y in range(0, chips, 2):
        q = jnp.concatenate([near[y, pairs:, :], near[y + 1, pairs:, :]], axis=0)
        total = jnp.zeros((8, both), jnp.float32)
        for j in range(0, chips, 2):
            items = jnp.concatenate([near[j, :pairs, :], near[j + 1, :pairs, :]], axis=0)
            e = jnp.exp(dot(items, q, NT) * scale_of(width))
            total = total + jnp.sum(e.reshape(both // 8, 8, both), axis=0)
        total = jnp.sum(total, axis=0, keepdims=True)
        sums_ref[y] = total[:, :pairs]
        sums_ref[y + 1] = total[:, pairs:]


def loss_body(
    y_ref, near, far, near_sums, normed_ref, factor_ref, item_w, query_w, hits_ref, more_hits_ref,
    loss_ref, grads_ref, more_grads_ref, inverse, own_exp,
):
    chips, both, width = near.shape
    pairs = both // 2
    scale = scale_of(width)
    own = y_ref[0]

    def items(y):
        return jnp.concatenate([near[y, :pairs, :], far[y, :pairs, :]], axis=0)

    def queries(y):
        return jnp.concatenate([near[y, pairs:, :], far[y, pairs:, :]], axis=0)

    def denominators(h, carry):
        y = 2 * h
        q = jnp.concatenate([queries(y), queries(y + 1)], axis=0)
        far_q = jnp.concatenate([far[y, pairs:, :], far[y + 1, pairs:, :]], axis=0)
        total = jnp.zeros((8, 2 * both), jnp.float32)
        far_total = jnp.zeros((8, both), jnp.float32)
        for j in range(0, chips, 2):
            far_items = jnp.concatenate([far[j, :pairs, :], far[j + 1, :pairs, :]], axis=0)
            near_items = jnp.concatenate([near[j, :pairs, :], near[j + 1, :pairs, :]], axis=0)
            e = jnp.exp(dot(far_items, q, NT) * scale)
            total = total + jnp.sum(e.reshape(both // 8, 8, 2 * both), axis=0)
            e = jnp.exp(dot(near_items, far_q, NT) * scale)
            far_total = far_total + jnp.sum(e.reshape(both // 8, 8, both), axis=0)
        total = jnp.sum(total, axis=0, keepdims=True)
        far_total = jnp.sum(far_total, axis=0, keepdims=True)
        for u in range(2):
            inverse[y + u] = jnp.concatenate(
                [
                    total[:, u * both : u * both + pairs] + near_sums[y + u],
                    total[:, u * both + pairs : (u + 1) * both] + far_total[:, u * pairs : (u + 1) * pairs],
                ],
                axis=1,
            )
        return carry

    lax.fori_loop(0, chips // 2, denominators, 0)
    item_own, query_own = near[own, :pairs, :], near[own, pairs:, :]
    own_hits = iota((pairs, pairs), 0) == iota((pairs, pairs), 1)
    diagonal = jnp.sum(
        jnp.where(own_hits, dot(item_own, query_own, NT) * scale, 0.0), axis=0, keepdims=True
    )
    loss_ref[...] = jnp.log(inverse[own][:, :pairs]) - diagonal
    ones = hits(iota((pairs, both), 0), iota((pairs, both), 1))
    grad_item = jnp.zeros((pairs, width), jnp.float32)
    row_total = jnp.zeros((pairs, LANES), jnp.float32)
    for y in range(chips):
        q = queries(y)
        soft = jnp.exp(dot(item_own, q, NT) * scale) * (1.0 / inverse[y])
        soft = soft - jnp.where(own == y, ones, 0.0)
        grad_item = grad_item + dot(soft.astype(jnp.bfloat16), q)
        e = jnp.exp(dot(query_own, items(y), NT) * scale)
        own_exp[y] = e
        for b in range(both // LANES):
            row_total = row_total + e[:, b * LANES : (b + 1) * LANES]
    row_inverse = 1.0 / jnp.sum(row_total, axis=1, keepdims=True)
    grad_query = jnp.zeros((pairs, width), jnp.float32)
    for y in range(chips):
        soft = own_exp[y] * row_inverse - jnp.where(own == y, ones, 0.0)
        grad_query = grad_query + dot(soft.astype(jnp.bfloat16), items(y))
    backs = []
    for side, (grad, w_ref) in enumerate(((grad_item, item_w), (grad_query, query_w))):
        span = pl.ds(side * pairs, pairs)
        grad = grad * scale
        normed = normed_ref[span, :]
        factor = factor_ref[span, 0:1]
        inner_mean = jnp.mean(grad * normed, axis=1, keepdims=True)
        grad_hidden = (factor * (grad - normed * inner_mean)).astype(jnp.bfloat16)
        backs.append(dot(grad_hidden, w_ref[...], NT))
    back = jnp.concatenate(backs, axis=0)
    high = back.astype(jnp.bfloat16)
    low = (back - high.astype(jnp.float32)).astype(jnp.bfloat16)
    step = 256
    for weights, out in ((hits_ref, grads_ref), (more_hits_ref, more_grads_ref)):
        for s in range(weights.shape[1] // step):
            weight = weights[:, s * step : (s + 1) * step]
            out[s * step : (s + 1) * step, :] = (
                dot(weight, high, TN) + dot(weight, low, TN)
            ).astype(jnp.bfloat16)


def column_body(codes_ref, more_codes_ref, grads_ref, more_grads_ref, out_ref, *, side):
    chips, per = out_ref.shape[:2]
    for y in range(0, chips, 2):
        begin = (side * chips + y) * per
        total = None
        for codes, grads in ((codes_ref, grads_ref), (more_codes_ref, more_grads_ref)):
            down = iota((2 * per, codes.shape[1]), 0)
            hot = hits(down, codes[...] - begin).astype(jnp.bfloat16)
            part = dot(hot, grads[...])
            total = part if total is None else total + part
        out_ref[y] = total[:per].astype(out_ref.dtype)
        out_ref[y + 1] = total[per:].astype(out_ref.dtype)


def add_body(a_ref, b_ref, out_ref):
    out_ref[...] = (a_ref[...] + b_ref[...].astype(jnp.float32)).astype(jnp.bfloat16)


def adagrad_body(parts_ref, table_ref, accum_ref, new_table_ref, new_accum_ref):
    grad = parts_ref[0].astype(jnp.float32)
    for y in range(1, parts_ref.shape[0]):
        grad = grad + parts_ref[y].astype(jnp.float32)
    rows, width = grad.shape
    mean = jnp.sum(grad * grad, axis=1, keepdims=True) * (1.0 / width)
    across = jnp.sum(
        jnp.where(iota((rows, rows), 0) == iota((rows, rows), 1), mean, 0.0), axis=0, keepdims=True
    )
    down = jnp.sum(
        jnp.where(iota((rows, rows), 0) == iota((rows, rows), 1), accum_ref[...], 0.0),
        axis=1,
        keepdims=True,
    )
    new_accum_ref[...] = accum_ref[...] + across
    new_table_ref[...] = table_ref[...] - learn_rate * grad / jnp.sqrt(down + mean)


def on_device(
    table, accum, item_weight, query_weight, packed_rows, block_counts, item_refs, query_refs
):
    bf16, f32, i32 = jnp.bfloat16, jnp.float32, jnp.int32
    shape = jax.ShapeDtypeStruct
    n_dp, n_table = lax.axis_size("dp"), lax.axis_size("table")
    chips = n_dp // CORES
    per, width = table.shape
    pairs = item_refs.shape[2]
    slots = CAP * n_dp
    base = slots * 3 // 4
    more = slots - base
    replica = lax.axis_index("dp")
    core = (replica % CORES).reshape(1).astype(i32)
    chip = (replica // CORES).reshape(1).astype(i32)
    along_y = [[y * CORES + c for y in range(chips)] for c in range(CORES)]
    swap = [(r, r ^ 1) for r in range(n_dp)]

    def over_y(x):
        return lax.all_to_all(
            x, "dp", split_axis=0, concat_axis=0, axis_index_groups=along_y, tiled=True
        )

    def over_table(x):
        parts = x.reshape(n_table, -1, x.shape[-1])
        return lax.all_to_all(parts, "table", split_axis=0, concat_axis=0, tiled=True).reshape(x.shape)

    near_rows = over_y(jnp.broadcast_to(table.astype(bf16)[None], (chips, per, width)))
    far_rows = lax.ppermute(near_rows, "dp", swap)
    items, queries = item_refs[0, 0].T, query_refs[0, 0].T
    requests, places = call(
        functools.partial(request_body, base=base),
        (shape((n_table, slots + 8), i32), shape((n_table, slots), i32)),
        [SMEM] + [VMEM] * 4,
        [
            pltpu.VMEM((32, LANES), f32),
            pltpu.VMEM((n_dp * n_table // LANES, LANES), f32),
            pltpu.VMEM((LANES, LANES), f32),
        ],
    )(core, packed_rows.reshape(1, -1), block_counts.reshape(1, -1), items, queries)
    received = over_table(requests)

    def pick(first, count):
        return call(
            functools.partial(pick_body, first=first, count=count, slots=slots),
            (shape((n_table * count, width), bf16), shape((1,), i32)),
            [VMEM] * 3,
            [pltpu.VMEM((LANES, LANES), f32)],
            out_specs=(VMEM, SMEM),
        )(received, near_rows, far_rows)

    picked, over = pick(0, base)
    fetched = over_table(picked)
    crowded = over[0] > 0
    nothing = jnp.zeros((n_table * more, width), bf16)
    more_fetched = lax.cond(
        crowded, lambda: over_table(pick(base, more)[0]), lambda: nothing
    )
    pair_hits, more_hits, normed, factor, spread = call(
        tower_body,
        (
            shape((2 * pairs, n_table * base), bf16),
            shape((2 * pairs, n_table * more), bf16),
            shape((2 * pairs, width), f32),
            shape((2 * pairs, LANES), f32),
            shape((chips, 2 * pairs, width), bf16),
        ),
        [VMEM] * 8,
        [pltpu.VMEM((LANES, LANES), f32)],
    )(
        places[:, :base].reshape(1, -1),
        places[:, base:].reshape(1, -1),
        items,
        queries,
        fetched,
        more_fetched,
        item_weight,
        query_weight,
    )
    near = over_y(spread)
    far = lax.ppermute(near, "dp", swap)
    near_sums = call(near_body, shape((chips, 1, pairs), f32), [VMEM])(near)
    loss, grads, more_grads = call(
        loss_body,
        (
            shape((1, pairs), f32),
            shape((n_table * base, width), bf16),
            shape((n_table * more, width), bf16),
        ),
        [SMEM] + [VMEM] * 9,
        [pltpu.VMEM((chips, 1, 2 * pairs), f32), pltpu.VMEM((chips, pairs, 2 * pairs), f32)],
    )(chip, near, far, near_sums, normed, factor, item_weight, query_weight, pair_hits, more_hits)
    returned = over_table(grads)
    more_returned = lax.cond(crowded, lambda: over_table(more_grads), lambda: nothing)
    codes = received[:, :base].reshape(1, -1)
    more_codes = received[:, base:slots].reshape(1, -1)

    def column(side, dtype):
        return call(
            functools.partial(column_body, side=side), shape((chips, per, width), dtype), [VMEM] * 4
        )(codes, more_codes, returned, more_returned)

    other = lax.ppermute(column(1, bf16), "dp", swap)
    both = call(add_body, shape((chips, per, width), bf16), [VMEM] * 2)(column(0, f32), other)
    new_table, new_accum = call(
        adagrad_body, (shape((per, width), f32), shape((1, per), f32)), [VMEM] * 3
    )(over_y(both), table, accum.reshape(1, per))
    return (new_table, new_accum.reshape(per), loss.reshape(1, 1, pairs))


def solution(mesh):
    in_specs = (
        P(("dp", "table"), None),
        P(("dp", "table")),
        P(),
        P(),
        P("dp", "table", None),
        P("dp", "table", None),
        P("dp", "table", None, None),
        P("dp", "table", None, None),
    )
    out_specs = (P(("dp", "table"), None), P(("dp", "table")), P("dp", "table", None))
    return jax.shard_map(
        on_device, mesh=mesh, in_specs=in_specs, out_specs=out_specs, check_vma=False
    )
```

```python
import functools
import math

import jax
import jax.numpy as jnp
from jax import lax
from jax.experimental import pallas as pl
from jax.experimental.pallas import tpu as pltpu
from jax.sharding import PartitionSpec as P

CAP = 2
LANES = 128
CORES = 2

learn_rate = 0.3
epsilon = 1e-06
sharpness = 3.0

VMEM = pl.BlockSpec(memory_space=pltpu.VMEM)
SMEM = pl.BlockSpec(memory_space=pltpu.SMEM)

NT = (((1,), (1,)), ((), ()))


def iota(shape, axis):
    return lax.broadcasted_iota(jnp.int32, shape, axis)


def dot(a, b, dims=(((1,), (0,)), ((), ()))):
    return lax.dot_general(a, b, dims, preferred_element_type=jnp.float32)


def hits(a, b):
    return jnp.where(a == b, 1.0, 0.0)


def call(body, out_shape, in_specs, scratch=(), out_specs=None):
    return pl.pallas_call(
        body,
        out_shape=out_shape,
        in_specs=in_specs,
        out_specs=jax.tree.map(lambda _: VMEM, out_shape) if out_specs is None else out_specs,
        scratch_shapes=list(scratch),
        compiler_params=pltpu.CompilerParams(vmem_limit_bytes=12 * 1024 * 1024),
    )


def request_body(
    core_ref, list_ref, counts_ref, item_refs, query_refs, accum_ref,
    req_ref, pos_ref, accum_out, looked, counts2d, square, *, base,
):
    length, owners = list_ref.shape[1], counts_ref.shape[1]
    rows = owners // LANES
    depth = looked.shape[0] // 2
    groups, slots = pos_ref.shape
    accum_out[...] = accum_ref[...]
    looked[...] = jnp.zeros_like(looked)
    for b in range(length // LANES):
        looked[b : b + 1, :] = list_ref[:, b * LANES : (b + 1) * LANES].astype(jnp.float32)
    for b in range(rows):
        counts2d[b : b + 1, :] = counts_ref[:, b * LANES : (b + 1) * LANES].astype(jnp.float32)
    down = iota((LANES, LANES), 0)
    block = iota((depth, LANES), 0)
    wanted = jnp.zeros((depth, LANES), jnp.float32)
    for refs_ref in (item_refs, query_refs):
        for l in range(refs_ref.shape[0]):
            ref = refs_ref[l : l + 1, :]
            high = hits(block, ref >> 7).astype(jnp.bfloat16)
            low = hits(down, ref & (LANES - 1)).astype(jnp.bfloat16)
            wanted = wanted + dot(high, low, NT)
    looked[depth:, :] = jnp.where(wanted > 0.5, 1.0, 0.0)
    looked_bf = looked[...].astype(jnp.bfloat16)

    counts = counts2d[...]
    counts_bf = counts.astype(jnp.bfloat16)
    before = hits(down < iota((LANES, LANES), 1), True).astype(jnp.bfloat16)
    within = dot(counts_bf, before)
    row_total = dot(counts_bf, jnp.ones((LANES, LANES), jnp.bfloat16))
    offsets = [jnp.zeros((1, LANES), jnp.float32)]
    for i in range(rows - 1):
        offsets.append(offsets[-1] + row_total[i : i + 1, :])
    starts = within + jnp.concatenate(offsets, axis=0)
    second = jnp.where(counts > 1.5, starts + 1.0, -1.0)
    positions = jnp.concatenate([starts, second], axis=0)
    pos_int = positions.astype(jnp.int32)
    entries = CAP * rows
    width = LANES // CORES
    owner_core = jnp.where(iota((1, LANES), 1) < width, 0, 1)
    side = jnp.where(owner_core == core_ref[0], 0.0, 1.0)
    square[...] = jnp.zeros_like(square)
    square[entries : 2 * entries, :] = positions
    for r in range(entries):
        p = pos_int[r : r + 1, :]
        spread = dot(looked_bf, hits(down, p & (LANES - 1)).astype(jnp.bfloat16))
        here = block == (p >> 7)
        value = jnp.sum(jnp.where(here, spread[:depth], 0.0), axis=0, keepdims=True)
        used = jnp.sum(jnp.where(here, spread[depth:], 0.0), axis=0, keepdims=True)
        square[r : r + 1, :] = value + (side * rows + (r % rows)) * LANES
        square[2 * entries + r : 2 * entries + r + 1, :] = used
    turned = square[...].T

    def column(n):
        part = slice(n * entries, (n + 1) * entries)
        return jnp.concatenate([turned[:width, part], turned[width:, part]], axis=1)

    codes, places, used = column(0), column(1), column(2)
    before = hits(iota((slots, slots), 0) < iota((slots, slots), 1), True).astype(jnp.bfloat16)
    rank = dot(used.astype(jnp.bfloat16), before)
    rank = jnp.where(used > 0.5, rank, -1.0).astype(jnp.int32)
    slot = iota((groups, slots), 1)
    packed_codes = jnp.full((groups, slots), -1.0, jnp.float32)
    packed_places = packed_codes
    for k in range(slots):
        here = slot == rank[:, k : k + 1]
        packed_codes = jnp.where(here, codes[:, k : k + 1], packed_codes)
        packed_places = jnp.where(here, places[:, k : k + 1], packed_places)
    over = jnp.max(rank, axis=1, keepdims=True)
    over = jnp.max(over, axis=0, keepdims=True)
    over = jnp.where(over >= base, 1, 0)
    pos_ref[...] = packed_places.astype(jnp.int32)
    req_ref[:, :slots] = packed_codes.astype(jnp.int32)
    req_ref[:, slots:] = jnp.broadcast_to(over, (groups, req_ref.shape[1] - slots))


def pick_body(recv_ref, near_ref, far_ref, out_ref, over_ref, square, *, first, count, slots):
    groups = recv_ref.shape[0]
    chips, per, width = near_ref.shape
    square[...] = jnp.zeros_like(square)
    square[:groups, : recv_ref.shape[1]] = recv_ref[...].astype(jnp.float32)
    turned = square[...].T.astype(jnp.int32)
    over_ref[0] = jnp.max(turned[slots : slots + 1, :groups])
    lane = iota((count, LANES), 1)
    rows = jnp.concatenate(
        [near_ref[...].reshape(chips * per, width), far_ref[...].reshape(chips * per, width)], axis=0
    )
    step = 8
    for t in range(0, groups, step):
        hot = []
        for u in range(t, t + step):
            code = jnp.broadcast_to(turned[first : first + count, u : u + 1], (count, LANES))
            hot.append(
                jnp.concatenate(
                    [hits(lane + b * LANES, code) for b in range(rows.shape[0] // LANES)], axis=1
                )
            )
        hot = jnp.concatenate(hot, axis=0).astype(jnp.bfloat16)
        out_ref[t * count : (t + step) * count, :] = dot(hot, rows).astype(jnp.bfloat16)


def project(pool, weight):
    hidden = dot(pool, weight)
    factor = lax.rsqrt(jnp.mean(hidden * hidden, axis=1, keepdims=True) + epsilon)
    return hidden * factor, factor


def pair_weight(refs, pos):
    weight = hits(refs[:, 0:1], pos)
    for l in range(1, refs.shape[1]):
        weight = weight + hits(refs[:, l : l + 1], pos)
    return weight.astype(jnp.bfloat16)


def tower_body(
    pos_ref, more_pos_ref, item_refs, query_refs, fetched, more_fetched, weights,
    hits_ref, more_hits_ref, pool_ref, out_ref, square,
):
    pairs = item_refs.shape[1]
    square[...] = jnp.zeros_like(square)
    square[0 : item_refs.shape[0], :] = item_refs[...].astype(jnp.float32)
    square[8 : 8 + query_refs.shape[0], :] = query_refs[...].astype(jnp.float32)
    turned = square[...].T.astype(jnp.int32)
    item_columns = turned[:, 0 : item_refs.shape[0]]
    query_columns = turned[:, 8 : 8 + query_refs.shape[0]]
    outs = []
    for side, refs in enumerate((item_columns, query_columns)):
        span = pl.ds(side * pairs, pairs)
        weight = pair_weight(refs, pos_ref[...])
        more_weight = pair_weight(refs, more_pos_ref[...])
        hits_ref[span, :] = weight
        more_hits_ref[span, :] = more_weight
        pool = (dot(weight, fetched[...]) + dot(more_weight, more_fetched[...])).astype(jnp.bfloat16)
        pool_ref[span, :] = pool
        outs.append(project(pool, weights[side])[0].astype(jnp.bfloat16))
    for y in range(out_ref.shape[0]):
        out_ref[y, :pairs, :] = outs[0]
        out_ref[y, pairs:, :] = outs[1]


def scale_of(width):
    return sharpness * width ** (-0.5)


def exp_of(products, width):
    return jnp.exp2(products * (scale_of(width) * math.log2(math.e)))


def near_body(near, hits_ref, more_hits_ref, sums_ref, turned_ref, more_turned_ref):
    chips, both, width = near.shape
    pairs = both // 2
    step = 256
    for weights, out in ((hits_ref, turned_ref), (more_hits_ref, more_turned_ref)):
        for s in range(0, weights.shape[1], step):
            out[s : s + step, :] = weights[:, s : s + step].T
    for y in range(0, chips, 2):
        q = jnp.concatenate([near[y, pairs:, :], near[y + 1, pairs:, :]], axis=0)
        total = jnp.zeros((8, both), jnp.float32)
        for j in range(0, chips, 2):
            items = jnp.concatenate([near[j, :pairs, :], near[j + 1, :pairs, :]], axis=0)
            e = exp_of(dot(items, q, NT), width)
            total = total + jnp.sum(e.reshape(both // 8, 8, both), axis=0)
        total = jnp.sum(total, axis=0, keepdims=True)
        sums_ref[y] = total[:, :pairs]
        sums_ref[y + 1] = total[:, pairs:]


def loss_body(
    y_ref, near, far, near_sums, pool_ref, weights_ref, turned_ref, more_turned_ref,
    loss_ref, grads_ref, more_grads_ref, inverse, own_exp,
):
    chips, both, width = near.shape
    pairs = both // 2
    scale = scale_of(width)
    own = y_ref[0]

    def items(y):
        return jnp.concatenate([near[y, :pairs, :], far[y, :pairs, :]], axis=0)

    def queries(y):
        return jnp.concatenate([near[y, pairs:, :], far[y, pairs:, :]], axis=0)

    def denominators(h, carry):
        y = 2 * h
        q = jnp.concatenate([queries(y), queries(y + 1)], axis=0)
        far_q = jnp.concatenate([far[y, pairs:, :], far[y + 1, pairs:, :]], axis=0)
        total = jnp.zeros((8, 2 * both), jnp.float32)
        far_total = jnp.zeros((8, both), jnp.float32)
        for j in range(0, chips, 2):
            far_items = jnp.concatenate([far[j, :pairs, :], far[j + 1, :pairs, :]], axis=0)
            near_items = jnp.concatenate([near[j, :pairs, :], near[j + 1, :pairs, :]], axis=0)
            e = exp_of(dot(far_items, q, NT), width)
            total = total + jnp.sum(e.reshape(both // 8, 8, 2 * both), axis=0)
            e = exp_of(dot(near_items, far_q, NT), width)
            far_total = far_total + jnp.sum(e.reshape(both // 8, 8, both), axis=0)
        total = jnp.sum(total, axis=0, keepdims=True)
        far_total = jnp.sum(far_total, axis=0, keepdims=True)
        for u in range(2):
            inverse[y + u] = jnp.concatenate(
                [
                    total[:, u * both : u * both + pairs] + near_sums[y + u],
                    total[:, u * both + pairs : (u + 1) * both] + far_total[:, u * pairs : (u + 1) * pairs],
                ],
                axis=1,
            )
        return carry

    for h in range(chips // 2):
        denominators(h, 0)
    item_own, query_own = near[own, :pairs, :], near[own, pairs:, :]
    own_hits = iota((pairs, pairs), 0) == iota((pairs, pairs), 1)
    diagonal = jnp.sum(
        jnp.where(own_hits, dot(item_own, query_own, NT) * scale, 0.0), axis=0, keepdims=True
    )
    loss_ref[...] = jnp.log(inverse[own][:, :pairs]) - diagonal
    ones = hits(iota((pairs, both), 0), iota((pairs, both), 1))
    grad_item = jnp.zeros((pairs, width), jnp.float32)
    row_total = jnp.zeros((pairs, LANES), jnp.float32)
    for y in range(chips):
        q = queries(y)
        soft = exp_of(dot(item_own, q, NT), width) * (1.0 / inverse[y])
        soft = soft - jnp.where(own == y, ones, 0.0)
        grad_item = grad_item + dot(soft.astype(jnp.bfloat16), q)
        e = exp_of(dot(query_own, items(y), NT), width)
        own_exp[y] = e
        for b in range(both // LANES):
            row_total = row_total + e[:, b * LANES : (b + 1) * LANES]
    row_inverse = 1.0 / jnp.sum(row_total, axis=1, keepdims=True)
    grad_query = jnp.zeros((pairs, width), jnp.float32)
    for y in range(chips):
        soft = own_exp[y] * row_inverse - jnp.where(own == y, ones, 0.0)
        grad_query = grad_query + dot(soft.astype(jnp.bfloat16), items(y))
    backs = []
    for side, grad in enumerate((grad_item, grad_query)):
        span = pl.ds(side * pairs, pairs)
        grad = grad * scale
        normed, factor = project(pool_ref[span, :], weights_ref[side])
        inner_mean = jnp.mean(grad * normed, axis=1, keepdims=True)
        grad_hidden = (factor * (grad - normed * inner_mean)).astype(jnp.bfloat16)
        backs.append(dot(grad_hidden, weights_ref[side], NT))
    back = jnp.concatenate(backs, axis=0)
    high = back.astype(jnp.bfloat16)
    low = (back - high.astype(jnp.float32)).astype(jnp.bfloat16)
    split = jnp.concatenate([high, low], axis=1)
    step = 256
    for weights, out in ((turned_ref, grads_ref), (more_turned_ref, more_grads_ref)):
        for s in range(0, weights.shape[0], step):
            parts = dot(weights[s : s + step, :], split)
            out[s : s + step, :] = (parts[:, :width] + parts[:, width:]).astype(jnp.bfloat16)


def column_body(codes_ref, more_codes_ref, grads_ref, more_grads_ref, out_ref, *, side):
    chips, per = out_ref.shape[:2]
    for y in range(0, chips, 2):
        begin = (side * chips + y) * per
        total = None
        for codes, grads in ((codes_ref, grads_ref), (more_codes_ref, more_grads_ref)):
            down = iota((2 * per, codes.shape[1]), 0)
            hot = hits(down, codes[...] - begin).astype(jnp.bfloat16)
            part = dot(hot, grads[...])
            total = part if total is None else total + part
        out_ref[y] = total[:per].astype(out_ref.dtype)
        out_ref[y + 1] = total[per:].astype(out_ref.dtype)


def add_body(a_ref, b_ref, out_ref):
    out_ref[...] = (a_ref[...] + b_ref[...].astype(jnp.float32)).astype(jnp.bfloat16)


def adagrad_body(parts_ref, table_ref, accum_ref, new_table_ref, new_accum_ref):
    grad = parts_ref[0].astype(jnp.float32)
    for y in range(1, parts_ref.shape[0]):
        grad = grad + parts_ref[y].astype(jnp.float32)
    rows, width = grad.shape
    mean = jnp.sum(grad * grad, axis=1, keepdims=True) * (1.0 / width)
    across = jnp.sum(
        jnp.where(iota((rows, rows), 0) == iota((rows, rows), 1), mean, 0.0), axis=0, keepdims=True
    )
    down = jnp.sum(
        jnp.where(iota((rows, rows), 0) == iota((rows, rows), 1), accum_ref[...], 0.0),
        axis=1,
        keepdims=True,
    )
    new_accum_ref[...] = accum_ref[...] + across
    new_table_ref[...] = table_ref[...] - learn_rate * grad / jnp.sqrt(down + mean)


def on_device(
    table, accum, item_weight, query_weight, packed_rows, block_counts, item_refs, query_refs
):
    bf16, f32, i32 = jnp.bfloat16, jnp.float32, jnp.int32
    shape = jax.ShapeDtypeStruct
    n_dp, n_table = lax.axis_size("dp"), lax.axis_size("table")
    chips = n_dp // CORES
    per, width = table.shape
    pairs = item_refs.shape[2]
    slots = CAP * n_dp
    base = slots * 3 // 4
    more = slots - base
    replica = lax.axis_index("dp")
    core = (replica % CORES).reshape(1).astype(i32)
    chip = (replica // CORES).reshape(1).astype(i32)
    along_y = [[y * CORES + c for y in range(chips)] for c in range(CORES)]
    swap = [(r, r ^ 1) for r in range(n_dp)]

    def over_y(x):
        return lax.all_to_all(
            x, "dp", split_axis=0, concat_axis=0, axis_index_groups=along_y, tiled=True
        )

    def over_table(x):
        parts = x.reshape(n_table, -1, x.shape[-1])
        return lax.all_to_all(parts, "table", split_axis=0, concat_axis=0, tiled=True).reshape(x.shape)

    near_rows = over_y(jnp.broadcast_to(table.astype(bf16)[None], (chips, per, width)))
    tower_weights = jnp.stack([item_weight, query_weight])
    items, queries = item_refs[0, 0].T, query_refs[0, 0].T
    requests, places, old_accum = call(
        functools.partial(request_body, base=base),
        (shape((n_table, slots + 8), i32), shape((n_table, slots), i32), shape((1, per), f32)),
        [SMEM] + [VMEM] * 5,
        [
            pltpu.VMEM((32, LANES), f32),
            pltpu.VMEM((n_dp * n_table // LANES, LANES), f32),
            pltpu.VMEM((LANES, LANES), f32),
        ],
    )(core, packed_rows.reshape(1, -1), block_counts.reshape(1, -1), items, queries, accum.reshape(1, per))
    near_rows, requests = lax.optimization_barrier((near_rows, requests))
    far_rows = lax.ppermute(near_rows, "dp", swap)
    received = over_table(requests)

    def pick(first, count, received):
        return call(
            functools.partial(pick_body, first=first, count=count, slots=slots),
            (shape((n_table * count, width), bf16), shape((1,), i32)),
            [VMEM] * 3,
            [pltpu.VMEM((LANES, LANES), f32)],
            out_specs=(VMEM, SMEM),
        )(received, near_rows, far_rows)

    picked, over = pick(0, base, received)
    fetched = over_table(picked)
    crowded = over[0] > 0
    nothing = jnp.zeros((n_table * more, width), bf16)
    late, fetched = lax.optimization_barrier((received, fetched))
    more_fetched = lax.cond(
        crowded, lambda: over_table(pick(base, more, late)[0]), lambda: nothing
    )
    pair_hits, more_hits, pool, spread = call(
        tower_body,
        (
            shape((2 * pairs, n_table * base), bf16),
            shape((2 * pairs, n_table * more), bf16),
            shape((2 * pairs, width), bf16),
            shape((chips, 2 * pairs, width), bf16),
        ),
        [VMEM] * 7,
        [pltpu.VMEM((LANES, LANES), f32)],
    )(
        places[:, :base].reshape(1, -1),
        places[:, base:].reshape(1, -1),
        items,
        queries,
        fetched,
        more_fetched,
        tower_weights,
    )
    near = over_y(spread)
    far = lax.ppermute(near, "dp", swap)
    near_sums, turned_hits, more_turned_hits = call(
        near_body,
        (
            shape((chips, 1, pairs), f32),
            shape((n_table * base, 2 * pairs), bf16),
            shape((n_table * more, 2 * pairs), bf16),
        ),
        [VMEM] * 3,
    )(near, pair_hits, more_hits)
    loss, grads, more_grads = call(
        loss_body,
        (
            shape((1, pairs), f32),
            shape((n_table * base, width), bf16),
            shape((n_table * more, width), bf16),
        ),
        [SMEM] + [VMEM] * 7,
        [pltpu.VMEM((chips, 1, 2 * pairs), f32), pltpu.VMEM((chips, pairs, 2 * pairs), f32)],
    )(chip, near, far, near_sums, pool, tower_weights, turned_hits, more_turned_hits)
    returned = over_table(grads)
    more_returned = lax.cond(crowded, lambda: over_table(more_grads), lambda: nothing)
    codes = received[:, :base].reshape(1, -1)
    more_codes = received[:, base:slots].reshape(1, -1)

    def column(side, dtype):
        return call(
            functools.partial(column_body, side=side), shape((chips, per, width), dtype), [VMEM] * 4
        )(codes, more_codes, returned, more_returned)

    other = lax.ppermute(column(1, bf16), "dp", swap)
    both = call(add_body, shape((chips, per, width), bf16), [VMEM] * 2)(column(0, f32), other)
    new_table, new_accum = call(
        adagrad_body, (shape((per, width), f32), shape((1, per), f32)), [VMEM] * 3
    )(over_y(both), table, old_accum)
    return (new_table, new_accum.reshape(per), loss.reshape(1, 1, pairs))


def solution(mesh):
    in_specs = (
        P(("dp", "table"), None),
        P(("dp", "table")),
        P(),
        P(),
        P("dp", "table", None),
        P("dp", "table", None),
        P("dp", "table", None, None),
        P("dp", "table", None, None),
    )
    out_specs = (P(("dp", "table"), None), P(("dp", "table")), P("dp", "table", None))
    return jax.shard_map(
        on_device, mesh=mesh, in_specs=in_specs, out_specs=out_specs, check_vma=False
    )
```

```python
import functools
import math

import jax
import jax.numpy as jnp
from jax import lax
from jax.experimental import pallas as pl
from jax.experimental.pallas import tpu as pltpu
from jax.sharding import PartitionSpec as P

CAP = 2
LANES = 128
CORES = 2

learn_rate = 0.3
epsilon = 1e-06
sharpness = 3.0

VMEM = pl.BlockSpec(memory_space=pltpu.VMEM)
SMEM = pl.BlockSpec(memory_space=pltpu.SMEM)

NT = (((1,), (1,)), ((), ()))


def iota(shape, axis):
    return lax.broadcasted_iota(jnp.int32, shape, axis)


def dot(a, b, dims=(((1,), (0,)), ((), ()))):
    return lax.dot_general(a, b, dims, preferred_element_type=jnp.float32)


def hits(a, b):
    return jnp.where(a == b, 1.0, 0.0)


def call(body, out_shape, in_specs, scratch=(), out_specs=None):
    return pl.pallas_call(
        body,
        out_shape=out_shape,
        in_specs=in_specs,
        out_specs=jax.tree.map(lambda _: VMEM, out_shape) if out_specs is None else out_specs,
        scratch_shapes=list(scratch),
        compiler_params=pltpu.CompilerParams(vmem_limit_bytes=12 * 1024 * 1024),
    )


def request_body(
    place_ref, list_ref, counts_ref, item_refs, query_refs, accum_ref,
    req_ref, pos_ref, accum_out, looked, counts2d, square, *, base,
):
    length, owners = list_ref.shape[1], counts_ref.shape[1]
    rows = owners // LANES
    depth = looked.shape[0] // 2
    groups, slots = pos_ref.shape
    accum_out[...] = accum_ref[...]
    looked[...] = jnp.zeros_like(looked)
    for b in range(length // LANES):
        looked[b : b + 1, :] = list_ref[:, b * LANES : (b + 1) * LANES].astype(jnp.float32)
    for b in range(rows):
        counts2d[b : b + 1, :] = counts_ref[:, b * LANES : (b + 1) * LANES].astype(jnp.float32)
    down = iota((LANES, LANES), 0)
    block = iota((depth, LANES), 0)
    wanted = jnp.zeros((depth, LANES), jnp.float32)
    for refs_ref in (item_refs, query_refs):
        for l in range(refs_ref.shape[0]):
            ref = refs_ref[l : l + 1, :]
            high = hits(block, ref >> 7).astype(jnp.bfloat16)
            low = hits(down, ref & (LANES - 1)).astype(jnp.bfloat16)
            wanted = wanted + dot(high, low, NT)
    looked[depth:, :] = jnp.where(wanted > 0.5, 1.0, 0.0)
    looked_bf = looked[...].astype(jnp.bfloat16)

    counts = counts2d[...]
    counts_bf = counts.astype(jnp.bfloat16)
    before = hits(down < iota((LANES, LANES), 1), True).astype(jnp.bfloat16)
    within = dot(counts_bf, before)
    row_total = dot(counts_bf, jnp.ones((LANES, LANES), jnp.bfloat16))
    offsets = [jnp.zeros((1, LANES), jnp.float32)]
    for i in range(rows - 1):
        offsets.append(offsets[-1] + row_total[i : i + 1, :])
    starts = within + jnp.concatenate(offsets, axis=0)
    second = jnp.where(counts > 1.5, starts + 1.0, -1.0)
    positions = jnp.concatenate([starts, second], axis=0)
    pos_int = positions.astype(jnp.int32)
    entries = CAP * rows
    width = LANES // CORES
    owner_core = jnp.where(iota((1, LANES), 1) < width, 0, 1)
    side = jnp.where(owner_core == place_ref[1], 0.0, 1.0)
    parity = place_ref[0] % 2
    square[...] = jnp.zeros_like(square)
    square[entries : 2 * entries, :] = positions
    for r in range(entries):
        p = pos_int[r : r + 1, :]
        spread = dot(looked_bf, hits(down, p & (LANES - 1)).astype(jnp.bfloat16))
        here = block == (p >> 7)
        value = jnp.sum(jnp.where(here, spread[:depth], 0.0), axis=0, keepdims=True)
        used = jnp.sum(jnp.where(here, spread[depth:], 0.0), axis=0, keepdims=True)
        y = r % rows
        apart = jnp.where(parity == y % 2, 0, rows // 2).astype(jnp.float32)
        square[r : r + 1, :] = value + (side * rows + apart + y // 2) * LANES
        square[2 * entries + r : 2 * entries + r + 1, :] = used
    turned = square[...].T

    def column(n):
        part = slice(n * entries, (n + 1) * entries)
        return jnp.concatenate([turned[:width, part], turned[width:, part]], axis=1)

    codes, places, used = column(0), column(1), column(2)
    before = hits(iota((slots, slots), 0) < iota((slots, slots), 1), True).astype(jnp.bfloat16)
    rank = dot(used.astype(jnp.bfloat16), before)
    rank = jnp.where(used > 0.5, rank, -1.0).astype(jnp.int32)
    slot = iota((groups, slots), 1)
    packed_codes = jnp.full((groups, slots), -1.0, jnp.float32)
    packed_places = packed_codes
    for k in range(slots):
        here = slot == rank[:, k : k + 1]
        packed_codes = jnp.where(here, codes[:, k : k + 1], packed_codes)
        packed_places = jnp.where(here, places[:, k : k + 1], packed_places)
    over = jnp.max(rank, axis=1, keepdims=True)
    over = jnp.max(over, axis=0, keepdims=True)
    over = jnp.where(over >= base, 1, 0)
    pos_ref[...] = packed_places.astype(jnp.int32)
    req_ref[:, :slots] = packed_codes.astype(jnp.int32)
    req_ref[:, slots:] = jnp.broadcast_to(over, (groups, req_ref.shape[1] - slots))


def pick_rows(recv_ref, row_refs, square, first, count, begin):
    groups = recv_ref.shape[0]
    square[...] = jnp.zeros_like(square)
    square[:groups, : recv_ref.shape[1]] = recv_ref[...].astype(jnp.float32)
    turned = square[...].T.astype(jnp.int32)
    rows = jnp.concatenate([ref[...].reshape(-1, ref.shape[-1]) for ref in row_refs], axis=0)
    lane = iota((count, LANES), 1)
    step = 8
    for t in range(0, groups, step):
        hot = []
        for u in range(t, t + step):
            code = jnp.broadcast_to(turned[first : first + count, u : u + 1], (count, LANES))
            hot.append(
                jnp.concatenate(
                    [hits(lane + (begin + b * LANES), code) for b in range(rows.shape[0] // LANES)],
                    axis=1,
                )
            )
        hot = jnp.concatenate(hot, axis=0).astype(jnp.bfloat16)
        yield pl.ds(t * count, step * count), dot(hot, rows)


def pick_near_body(recv_ref, near_ref, next_ref, out_ref, square, *, first, count):
    for span, got in pick_rows(recv_ref, (near_ref, next_ref), square, first, count, 0):
        out_ref[span, :] = got.astype(jnp.bfloat16)


def pick_far_body(recv_ref, far_ref, near_got, out_ref, over_ref, square, *, first, count, slots):
    begin = far_ref.shape[0] * far_ref.shape[1]
    for span, got in pick_rows(recv_ref, (far_ref,), square, first, count, begin):
        out_ref[span, :] = (got + near_got[span, :].astype(jnp.float32)).astype(jnp.bfloat16)
    over_ref[0] = jnp.max(recv_ref[:, slots : slots + 1])


def project(pool, weight):
    hidden = dot(pool, weight)
    factor = lax.rsqrt(jnp.mean(hidden * hidden, axis=1, keepdims=True) + epsilon)
    return hidden * factor, factor


def pair_weight(refs, pos):
    weight = hits(refs[:, 0:1], pos)
    for l in range(1, refs.shape[1]):
        weight = weight + hits(refs[:, l : l + 1], pos)
    return weight.astype(jnp.bfloat16)


def tower_body(
    recv_ref, pos_ref, more_pos_ref, item_refs, query_refs, fetched, more_fetched, weights,
    hits_ref, more_hits_ref, pool_ref, out_ref, square, pool_sum, more_rows, sem,
):
    pairs = item_refs.shape[1]
    square[...] = jnp.zeros_like(square)
    square[0 : item_refs.shape[0], :] = item_refs[...].astype(jnp.float32)
    square[8 : 8 + query_refs.shape[0], :] = query_refs[...].astype(jnp.float32)
    turned = square[...].T.astype(jnp.int32)
    item_columns = turned[:, 0 : item_refs.shape[0]]
    query_columns = turned[:, 8 : 8 + query_refs.shape[0]]
    slots = (pos_ref.shape[1] + more_pos_ref.shape[1]) // recv_ref.shape[0]
    crowded = jnp.max(recv_ref[:, slots : slots + 1]) > 0
    spans = [pl.ds(side * pairs, pairs) for side in range(2)]
    for span, refs in zip(spans, (item_columns, query_columns)):
        weight = pair_weight(refs, pos_ref[...])
        hits_ref[span, :] = weight
        pool_sum[span, :] = dot(weight, fetched[...])
    more_hits_ref[...] = jnp.zeros_like(more_hits_ref)

    @pl.when(crowded)
    def _():
        copy = pltpu.make_async_copy(more_fetched, more_rows, sem)
        copy.start()
        copy.wait()
        for span, refs in zip(spans, (item_columns, query_columns)):
            weight = pair_weight(refs, more_pos_ref[...])
            more_hits_ref[span, :] = weight
            pool_sum[span, :] = pool_sum[span, :] + dot(weight, more_rows[...])

    outs = []
    for side, span in enumerate(spans):
        pool = pool_sum[span, :].astype(jnp.bfloat16)
        pool_ref[span, :] = pool
        outs.append(project(pool, weights[side])[0].astype(jnp.bfloat16))
    for y in range(out_ref.shape[0]):
        out_ref[y, :pairs, :] = outs[0]
        out_ref[y, pairs:, :] = outs[1]


def scale_of(width):
    return sharpness * width ** (-0.5)


def exp_of(products, width):
    return jnp.exp2(products * (scale_of(width) * math.log2(math.e)))


def near_body(near, hits_ref, more_hits_ref, sums_ref, turned_ref, more_turned_ref):
    chips, both, width = near.shape
    pairs = both // 2
    step = 256
    for weights, out in ((hits_ref, turned_ref), (more_hits_ref, more_turned_ref)):
        for s in range(0, weights.shape[1], step):
            out[s : s + step, :] = weights[:, s : s + step].T
    for y in range(0, chips, 2):
        q = jnp.concatenate([near[y, pairs:, :], near[y + 1, pairs:, :]], axis=0)
        total = jnp.zeros((8, both), jnp.float32)
        for j in range(0, chips, 2):
            items = jnp.concatenate([near[j, :pairs, :], near[j + 1, :pairs, :]], axis=0)
            e = exp_of(dot(items, q, NT), width)
            total = total + jnp.sum(e.reshape(both // 8, 8, both), axis=0)
        total = jnp.sum(total, axis=0, keepdims=True)
        sums_ref[y] = total[:, :pairs]
        sums_ref[y + 1] = total[:, pairs:]


def loss_body(
    y_ref, near, far, near_sums, pool_ref, weights_ref, turned_ref, more_turned_ref,
    loss_ref, grads_ref, more_grads_ref, inverse, own_exp,
):
    chips, both, width = near.shape
    pairs = both // 2
    scale = scale_of(width)
    own = y_ref[0]

    def items(y):
        return jnp.concatenate([near[y, :pairs, :], far[y, :pairs, :]], axis=0)

    def queries(y):
        return jnp.concatenate([near[y, pairs:, :], far[y, pairs:, :]], axis=0)

    def denominators(h, carry):
        y = 2 * h
        q = jnp.concatenate([queries(y), queries(y + 1)], axis=0)
        far_q = jnp.concatenate([far[y, pairs:, :], far[y + 1, pairs:, :]], axis=0)
        total = jnp.zeros((8, 2 * both), jnp.float32)
        far_total = jnp.zeros((8, both), jnp.float32)
        for j in range(0, chips, 2):
            far_items = jnp.concatenate([far[j, :pairs, :], far[j + 1, :pairs, :]], axis=0)
            near_items = jnp.concatenate([near[j, :pairs, :], near[j + 1, :pairs, :]], axis=0)
            e = exp_of(dot(far_items, q, NT), width)
            total = total + jnp.sum(e.reshape(both // 8, 8, 2 * both), axis=0)
            e = exp_of(dot(near_items, far_q, NT), width)
            far_total = far_total + jnp.sum(e.reshape(both // 8, 8, both), axis=0)
        total = jnp.sum(total, axis=0, keepdims=True)
        far_total = jnp.sum(far_total, axis=0, keepdims=True)
        for u in range(2):
            inverse[y + u] = jnp.concatenate(
                [
                    total[:, u * both : u * both + pairs] + near_sums[y + u],
                    total[:, u * both + pairs : (u + 1) * both] + far_total[:, u * pairs : (u + 1) * pairs],
                ],
                axis=1,
            )
        return carry

    for h in range(chips // 2):
        denominators(h, 0)
    item_own, query_own = near[own, :pairs, :], near[own, pairs:, :]
    own_hits = iota((pairs, pairs), 0) == iota((pairs, pairs), 1)
    diagonal = jnp.sum(
        jnp.where(own_hits, dot(item_own, query_own, NT) * scale, 0.0), axis=0, keepdims=True
    )
    loss_ref[...] = jnp.log(inverse[own][:, :pairs]) - diagonal
    ones = hits(iota((pairs, both), 0), iota((pairs, both), 1))
    grad_item = jnp.zeros((pairs, width), jnp.float32)
    row_total = jnp.zeros((pairs, LANES), jnp.float32)
    for y in range(chips):
        q = queries(y)
        soft = exp_of(dot(item_own, q, NT), width) * (1.0 / inverse[y])
        soft = soft - jnp.where(own == y, ones, 0.0)
        grad_item = grad_item + dot(soft.astype(jnp.bfloat16), q)
        e = exp_of(dot(query_own, items(y), NT), width)
        own_exp[y] = e
        for b in range(both // LANES):
            row_total = row_total + e[:, b * LANES : (b + 1) * LANES]
    row_inverse = 1.0 / jnp.sum(row_total, axis=1, keepdims=True)
    grad_query = jnp.zeros((pairs, width), jnp.float32)
    for y in range(chips):
        soft = own_exp[y] * row_inverse - jnp.where(own == y, ones, 0.0)
        grad_query = grad_query + dot(soft.astype(jnp.bfloat16), items(y))
    backs = []
    for side, grad in enumerate((grad_item, grad_query)):
        span = pl.ds(side * pairs, pairs)
        grad = grad * scale
        normed, factor = project(pool_ref[span, :], weights_ref[side])
        inner_mean = jnp.mean(grad * normed, axis=1, keepdims=True)
        grad_hidden = (factor * (grad - normed * inner_mean)).astype(jnp.bfloat16)
        backs.append(dot(grad_hidden, weights_ref[side], NT))
    back = jnp.concatenate(backs, axis=0)
    high = back.astype(jnp.bfloat16)
    low = (back - high.astype(jnp.float32)).astype(jnp.bfloat16)
    split = jnp.concatenate([high, low], axis=1)
    step = 256
    for weights, out in ((turned_ref, grads_ref), (more_turned_ref, more_grads_ref)):
        for s in range(0, weights.shape[0], step):
            parts = dot(weights[s : s + step, :], split)
            out[s : s + step, :] = (parts[:, :width] + parts[:, width:]).astype(jnp.bfloat16)


def column_body(
    place_ref, recv_ref, codes_ref, more_codes_ref, grads_ref, more_grads_ref, out_ref, sums, more_rows, sem, *, side
):
    chips, per = out_ref.shape[:2]
    slots = (codes_ref.shape[1] + more_codes_ref.shape[1]) // recv_ref.shape[0]
    crowded = jnp.max(recv_ref[:, slots : slots + 1]) > 0

    def sum_of(codes, grads, y):
        hot = hits(iota((2 * per, codes.shape[1]), 0), codes - (side * chips + y) * per)
        return dot(hot.astype(jnp.bfloat16), grads)

    for y in range(0, chips, 2):
        sums[y * per : (y + 2) * per, :] = sum_of(codes_ref[...], grads_ref[...], y)

    @pl.when(crowded)
    def _():
        copy = pltpu.make_async_copy(more_grads_ref, more_rows, sem)
        copy.start()
        copy.wait()
        for y in range(0, chips, 2):
            span = pl.ds(y * per, 2 * per)
            sums[span, :] = sums[span, :] + sum_of(more_codes_ref[...], more_rows[...], y)

    parity = place_ref[0] % 2
    for y in range(chips):
        half, k = divmod(y, chips // 2)
        owner_y = 2 * k + (parity if half == 0 else 1 - parity)
        out_ref[owner_y] = sums[y * per : (y + 1) * per, :].astype(out_ref.dtype)


def add_body(a_ref, b_ref, out_ref):
    out_ref[...] = (a_ref[...] + b_ref[...].astype(jnp.float32)).astype(jnp.bfloat16)


def adagrad_body(parts_ref, table_ref, accum_ref, new_table_ref, new_accum_ref):
    grad = parts_ref[0].astype(jnp.float32)
    for y in range(1, parts_ref.shape[0]):
        grad = grad + parts_ref[y].astype(jnp.float32)
    rows, width = grad.shape
    mean = jnp.sum(grad * grad, axis=1, keepdims=True) * (1.0 / width)
    across = jnp.sum(
        jnp.where(iota((rows, rows), 0) == iota((rows, rows), 1), mean, 0.0), axis=0, keepdims=True
    )
    down = jnp.sum(
        jnp.where(iota((rows, rows), 0) == iota((rows, rows), 1), accum_ref[...], 0.0),
        axis=1,
        keepdims=True,
    )
    new_accum_ref[...] = accum_ref[...] + across
    new_table_ref[...] = table_ref[...] - learn_rate * grad / jnp.sqrt(down + mean)


def on_device(
    table, accum, item_weight, query_weight, packed_rows, block_counts, item_refs, query_refs
):
    bf16, f32, i32 = jnp.bfloat16, jnp.float32, jnp.int32
    shape = jax.ShapeDtypeStruct
    n_dp, n_table = lax.axis_size("dp"), lax.axis_size("table")
    chips = n_dp // CORES
    per, width = table.shape
    pairs = item_refs.shape[2]
    slots = CAP * n_dp
    base = slots * 3 // 4
    more = slots - base
    replica = lax.axis_index("dp")
    place = jnp.stack([replica // CORES, replica % CORES]).astype(i32)
    along_y = [[y * CORES + c for y in range(chips)] for c in range(CORES)]
    along_parity = [
        [(2 * k + p) * CORES + c for k in range(chips // 2)] for p in range(2) for c in range(CORES)
    ]
    swap = [(r, r ^ 1) for r in range(n_dp)]
    beside = [
        (y * CORES + c, (y + (chips - 1 if c == 0 else 1)) % chips * CORES + c)
        for y in range(chips)
        for c in range(CORES)
    ]

    def over_y(x):
        return lax.all_to_all(
            x, "dp", split_axis=0, concat_axis=0, axis_index_groups=along_y, tiled=True
        )

    def over_table(x):
        parts = x.reshape(n_table, -1, x.shape[-1])
        return lax.all_to_all(parts, "table", split_axis=0, concat_axis=0, tiled=True).reshape(x.shape)

    near_rows = lax.all_to_all(
        jnp.broadcast_to(table.astype(bf16)[None], (chips // 2, per, width)),
        "dp",
        split_axis=0,
        concat_axis=0,
        axis_index_groups=along_parity,
        tiled=True,
    )
    tower_weights = jnp.stack([item_weight, query_weight])
    items, queries = item_refs[0, 0].T, query_refs[0, 0].T
    requests, places, old_accum = call(
        functools.partial(request_body, base=base),
        (shape((n_table, slots + 8), i32), shape((n_table, slots), i32), shape((1, per), f32)),
        [SMEM] + [VMEM] * 5,
        [
            pltpu.VMEM((32, LANES), f32),
            pltpu.VMEM((n_dp * n_table // LANES, LANES), f32),
            pltpu.VMEM((LANES, LANES), f32),
        ],
    )(place, packed_rows.reshape(1, -1), block_counts.reshape(1, -1), items, queries, accum.reshape(1, per))
    near_rows, requests = lax.optimization_barrier((near_rows, requests))
    next_rows = lax.ppermute(near_rows, "dp", beside)
    received = over_table(requests)
    received, near_rows, next_rows = lax.optimization_barrier((received, near_rows, next_rows))
    far_rows = lax.ppermute(jnp.concatenate([near_rows, next_rows]), "dp", swap)

    def pick(first, count, received):
        picked = shape((n_table * count, width), bf16)
        square = [pltpu.VMEM((LANES, LANES), f32)]
        near_got = call(
            functools.partial(pick_near_body, first=first, count=count), picked, [VMEM] * 3, square
        )(received, near_rows, next_rows)
        return call(
            functools.partial(pick_far_body, first=first, count=count, slots=slots),
            (picked, shape((1,), i32)),
            [VMEM] * 3,
            square,
            out_specs=(VMEM, SMEM),
        )(received, far_rows, near_got)

    picked, over = pick(0, base, received)
    fetched = over_table(picked)
    crowded = over[0] > 0
    nothing = jnp.zeros((n_table * more, width), bf16)
    late, fetched = lax.optimization_barrier((received, fetched))
    more_fetched = lax.cond(
        crowded, lambda: over_table(pick(base, more, late)[0]), lambda: nothing
    )
    pair_hits, more_hits, pool, spread = call(
        tower_body,
        (
            shape((2 * pairs, n_table * base), bf16),
            shape((2 * pairs, n_table * more), bf16),
            shape((2 * pairs, width), bf16),
            shape((chips, 2 * pairs, width), bf16),
        ),
        [VMEM] * 6 + [pl.BlockSpec(memory_space=pl.ANY), VMEM],
        [
            pltpu.VMEM((LANES, LANES), f32),
            pltpu.VMEM((2 * pairs, width), f32),
            pltpu.VMEM((n_table * more, width), bf16),
            pltpu.SemaphoreType.DMA,
        ],
    )(
        received,
        places[:, :base].reshape(1, -1),
        places[:, base:].reshape(1, -1),
        items,
        queries,
        fetched,
        more_fetched,
        tower_weights,
    )
    near = over_y(spread)
    far = lax.ppermute(near, "dp", swap)
    near_sums, turned_hits, more_turned_hits = call(
        near_body,
        (
            shape((chips, 1, pairs), f32),
            shape((n_table * base, 2 * pairs), bf16),
            shape((n_table * more, 2 * pairs), bf16),
        ),
        [VMEM] * 3,
    )(near, pair_hits, more_hits)
    loss, grads, more_grads = call(
        loss_body,
        (
            shape((1, pairs), f32),
            shape((n_table * base, width), bf16),
            shape((n_table * more, width), bf16),
        ),
        [SMEM] + [VMEM] * 7,
        [pltpu.VMEM((chips, 1, 2 * pairs), f32), pltpu.VMEM((chips, pairs, 2 * pairs), f32)],
    )(place, near, far, near_sums, pool, tower_weights, turned_hits, more_turned_hits)
    returned = over_table(grads)
    more_returned = lax.cond(crowded, lambda: over_table(more_grads), lambda: nothing)
    codes = received[:, :base].reshape(1, -1)
    more_codes = received[:, base:slots].reshape(1, -1)

    def column(side, dtype):
        return call(
            functools.partial(column_body, side=side),
            shape((chips, per, width), dtype),
            [SMEM] + [VMEM] * 4 + [pl.BlockSpec(memory_space=pl.ANY)],
            [
                pltpu.VMEM((chips * per, width), f32),
                pltpu.VMEM((n_table * more, width), bf16),
                pltpu.SemaphoreType.DMA,
            ],
        )(place, received, codes, more_codes, returned, more_returned)

    other = lax.ppermute(column(1, bf16), "dp", swap)
    both = call(add_body, shape((chips, per, width), bf16), [VMEM] * 2)(column(0, f32), other)
    new_table, new_accum = call(
        adagrad_body, (shape((per, width), f32), shape((1, per), f32)), [VMEM] * 3
    )(over_y(both), table, old_accum)
    return (new_table, new_accum.reshape(per), loss.reshape(1, 1, pairs))


def solution(mesh):
    in_specs = (
        P(("dp", "table"), None),
        P(("dp", "table")),
        P(),
        P(),
        P("dp", "table", None),
        P("dp", "table", None),
        P("dp", "table", None, None),
        P("dp", "table", None, None),
    )
    out_specs = (P(("dp", "table"), None), P(("dp", "table")), P("dp", "table", None))
    return jax.shard_map(
        on_device, mesh=mesh, in_specs=in_specs, out_specs=out_specs, check_vma=False
    )
```

```python
import functools
import math

import jax
import jax.numpy as jnp
from jax import lax
from jax.experimental import pallas as pl
from jax.experimental.pallas import tpu as pltpu
from jax.sharding import PartitionSpec as P

CAP = 2
LANES = 128
CORES = 2

learn_rate = 0.3
epsilon = 1e-06
sharpness = 3.0

VMEM = pl.BlockSpec(memory_space=pltpu.VMEM)
SMEM = pl.BlockSpec(memory_space=pltpu.SMEM)

NT = (((1,), (1,)), ((), ()))


def iota(shape, axis):
    return lax.broadcasted_iota(jnp.int32, shape, axis)


def dot(a, b, dims=(((1,), (0,)), ((), ()))):
    return lax.dot_general(a, b, dims, preferred_element_type=jnp.float32)


def hits(a, b):
    return jnp.where(a == b, 1.0, 0.0)


def call(body, out_shape, in_specs, scratch=(), out_specs=None):
    return pl.pallas_call(
        body,
        out_shape=out_shape,
        in_specs=in_specs,
        out_specs=jax.tree.map(lambda _: VMEM, out_shape) if out_specs is None else out_specs,
        scratch_shapes=list(scratch),
        compiler_params=pltpu.CompilerParams(vmem_limit_bytes=12 * 1024 * 1024),
    )


def request_body(
    y_ref, core_ref, list_ref, counts_ref, item_refs, query_refs, accum_ref,
    req_ref, pos_ref, accum_out, looked, counts2d, square, *, base,
):
    length, owners = list_ref.shape[1], counts_ref.shape[1]
    rows = owners // LANES
    depth = looked.shape[0] // 2
    groups, slots = pos_ref.shape
    accum_out[...] = accum_ref[...]
    looked[...] = jnp.zeros_like(looked)
    for b in range(length // LANES):
        looked[b : b + 1, :] = list_ref[:, b * LANES : (b + 1) * LANES].astype(jnp.float32)
    for b in range(rows):
        counts2d[b : b + 1, :] = counts_ref[:, b * LANES : (b + 1) * LANES].astype(jnp.float32)
    down = iota((LANES, LANES), 0)
    block = iota((depth, LANES), 0)
    wanted = jnp.zeros((depth, LANES), jnp.float32)
    for refs_ref in (item_refs, query_refs):
        for l in range(refs_ref.shape[0]):
            ref = refs_ref[l : l + 1, :]
            high = hits(block, ref >> 7).astype(jnp.bfloat16)
            low = hits(down, ref & (LANES - 1)).astype(jnp.bfloat16)
            wanted = wanted + dot(high, low, NT)
    looked[depth:, :] = jnp.where(wanted > 0.5, 1.0, 0.0)
    looked_bf = looked[...].astype(jnp.bfloat16)

    counts = counts2d[...]
    counts_bf = counts.astype(jnp.bfloat16)
    before = hits(down < iota((LANES, LANES), 1), True).astype(jnp.bfloat16)
    within = dot(counts_bf, before)
    row_total = dot(counts_bf, jnp.ones((LANES, LANES), jnp.bfloat16))
    offsets = [jnp.zeros((1, LANES), jnp.float32)]
    for i in range(rows - 1):
        offsets.append(offsets[-1] + row_total[i : i + 1, :])
    starts = within + jnp.concatenate(offsets, axis=0)
    second = jnp.where(counts > 1.5, starts + 1.0, -1.0)
    positions = jnp.concatenate([starts, second], axis=0)
    pos_int = positions.astype(jnp.int32)
    entries = CAP * rows
    width = LANES // CORES
    owner_core = jnp.where(iota((1, LANES), 1) < width, 0, 1)
    side = jnp.where(owner_core == core_ref[0], 0.0, 1.0)
    parity = y_ref[0] % 2
    square[...] = jnp.zeros_like(square)
    square[entries : 2 * entries, :] = positions
    for r in range(entries):
        p = pos_int[r : r + 1, :]
        spread = dot(looked_bf, hits(down, p & (LANES - 1)).astype(jnp.bfloat16))
        here = block == (p >> 7)
        value = jnp.sum(jnp.where(here, spread[:depth], 0.0), axis=0, keepdims=True)
        used = jnp.sum(jnp.where(here, spread[depth:], 0.0), axis=0, keepdims=True)
        y = r % rows
        apart = jnp.where(parity == y % 2, 0, rows // 2).astype(jnp.float32)
        square[r : r + 1, :] = value + ((apart + y // 2) * CORES + side) * LANES
        square[2 * entries + r : 2 * entries + r + 1, :] = used
    turned = square[...].T

    def column(n):
        part = slice(n * entries, (n + 1) * entries)
        return jnp.concatenate([turned[:width, part], turned[width:, part]], axis=1)

    codes, places, used = column(0), column(1), column(2)
    before = hits(iota((slots, slots), 0) < iota((slots, slots), 1), True).astype(jnp.bfloat16)
    rank = dot(used.astype(jnp.bfloat16), before)
    rank = jnp.where(used > 0.5, rank, -1.0).astype(jnp.int32)
    slot = iota((groups, slots), 1)
    packed_codes = jnp.full((groups, slots), -1.0, jnp.float32)
    packed_places = packed_codes
    for k in range(slots):
        here = slot == rank[:, k : k + 1]
        packed_codes = jnp.where(here, codes[:, k : k + 1], packed_codes)
        packed_places = jnp.where(here, places[:, k : k + 1], packed_places)
    over = jnp.max(rank, axis=1, keepdims=True)
    over = jnp.max(over, axis=0, keepdims=True)
    over = jnp.where(over >= base, 1, 0)
    pos_ref[...] = packed_places.astype(jnp.int32)
    req_ref[:, :slots] = packed_codes.astype(jnp.int32)
    req_ref[:, slots:] = jnp.broadcast_to(over, (groups, req_ref.shape[1] - slots))


def pick_body(recv_ref, near_ref, next_ref, out_ref, over_ref, square, *, first, count, slots):
    groups = recv_ref.shape[0]
    square[...] = jnp.zeros_like(square)
    square[:groups, : recv_ref.shape[1]] = recv_ref[...].astype(jnp.float32)
    turned = square[...].T.astype(jnp.int32)
    over_ref[0] = jnp.max(turned[slots : slots + 1, :groups])
    rows = jnp.concatenate([ref[...].reshape(-1, ref.shape[-1]) for ref in (near_ref, next_ref)], axis=0)
    lane = iota((count, LANES), 1)
    step = 8
    for t in range(0, groups, step):
        hot = []
        for u in range(t, t + step):
            code = jnp.broadcast_to(turned[first : first + count, u : u + 1], (count, LANES))
            hot.append(
                jnp.concatenate(
                    [hits(lane + b * LANES, code) for b in range(rows.shape[0] // LANES)], axis=1
                )
            )
        hot = jnp.concatenate(hot, axis=0).astype(jnp.bfloat16)
        out_ref[t * count : (t + step) * count, :] = dot(hot, rows).astype(jnp.bfloat16)


def project(pool, weight):
    hidden = dot(pool, weight)
    factor = lax.rsqrt(jnp.mean(hidden * hidden, axis=1, keepdims=True) + epsilon)
    return hidden * factor, factor


def pair_weight(refs, pos):
    weight = hits(refs[:, 0:1], pos)
    for l in range(1, refs.shape[1]):
        weight = weight + hits(refs[:, l : l + 1], pos)
    return weight.astype(jnp.bfloat16)


def tower_body(
    recv_ref, pos_ref, more_pos_ref, item_refs, query_refs, fetched, more_fetched, weights,
    hits_ref, more_hits_ref, pool_ref, out_ref, square, pool_sum, more_rows, sem,
):
    pairs = item_refs.shape[1]
    square[...] = jnp.zeros_like(square)
    square[0 : item_refs.shape[0], :] = item_refs[...].astype(jnp.float32)
    square[8 : 8 + query_refs.shape[0], :] = query_refs[...].astype(jnp.float32)
    turned = square[...].T.astype(jnp.int32)
    item_columns = turned[:, 0 : item_refs.shape[0]]
    query_columns = turned[:, 8 : 8 + query_refs.shape[0]]
    slots = (pos_ref.shape[1] + more_pos_ref.shape[1]) // recv_ref.shape[0]
    crowded = jnp.max(recv_ref[:, slots : slots + 1]) > 0
    spans = [pl.ds(side * pairs, pairs) for side in range(2)]
    for span, refs in zip(spans, (item_columns, query_columns)):
        weight = pair_weight(refs, pos_ref[...])
        hits_ref[span, :] = weight
        pool_sum[span, :] = dot(weight, fetched[...])
    more_hits_ref[...] = jnp.zeros_like(more_hits_ref)

    @pl.when(crowded)
    def _():
        copy = pltpu.make_async_copy(more_fetched, more_rows, sem)
        copy.start()
        copy.wait()
        for span, refs in zip(spans, (item_columns, query_columns)):
            weight = pair_weight(refs, more_pos_ref[...])
            more_hits_ref[span, :] = weight
            pool_sum[span, :] = pool_sum[span, :] + dot(weight, more_rows[...])

    outs = []
    for side, span in enumerate(spans):
        pool = pool_sum[span, :].astype(jnp.bfloat16)
        pool_ref[span, :] = pool
        outs.append(project(pool, weights[side])[0].astype(jnp.bfloat16))
    for y in range(out_ref.shape[0]):
        out_ref[y, :pairs, :] = outs[0]
        out_ref[y, pairs:, :] = outs[1]


def scale_of(width):
    return sharpness * width ** (-0.5)


def exp_of(products, width):
    return jnp.exp2(products * (scale_of(width) * math.log2(math.e)))


def near_body(near, hits_ref, more_hits_ref, sums_ref, turned_ref, more_turned_ref):
    chips, both, width = near.shape
    pairs = both // 2
    step = 256
    for weights, out in ((hits_ref, turned_ref), (more_hits_ref, more_turned_ref)):
        for s in range(0, weights.shape[1], step):
            out[s : s + step, :] = weights[:, s : s + step].T
    for y in range(0, chips, 2):
        q = jnp.concatenate([near[y, pairs:, :], near[y + 1, pairs:, :]], axis=0)
        total = jnp.zeros((8, both), jnp.float32)
        for j in range(0, chips, 2):
            items = jnp.concatenate([near[j, :pairs, :], near[j + 1, :pairs, :]], axis=0)
            e = exp_of(dot(items, q, NT), width)
            total = total + jnp.sum(e.reshape(both // 8, 8, both), axis=0)
        total = jnp.sum(total, axis=0, keepdims=True)
        sums_ref[y] = total[:, :pairs]
        sums_ref[y + 1] = total[:, pairs:]


def loss_body(
    y_ref, near, far, near_sums, pool_ref, weights_ref, turned_ref, more_turned_ref,
    loss_ref, grads_ref, more_grads_ref, inverse, own_exp,
):
    chips, both, width = near.shape
    pairs = both // 2
    scale = scale_of(width)
    own = y_ref[0]

    def items(y):
        return jnp.concatenate([near[y, :pairs, :], far[y, :pairs, :]], axis=0)

    def queries(y):
        return jnp.concatenate([near[y, pairs:, :], far[y, pairs:, :]], axis=0)

    def denominators(h, carry):
        y = 2 * h
        q = jnp.concatenate([queries(y), queries(y + 1)], axis=0)
        far_q = jnp.concatenate([far[y, pairs:, :], far[y + 1, pairs:, :]], axis=0)
        total = jnp.zeros((8, 2 * both), jnp.float32)
        far_total = jnp.zeros((8, both), jnp.float32)
        for j in range(0, chips, 2):
            far_items = jnp.concatenate([far[j, :pairs, :], far[j + 1, :pairs, :]], axis=0)
            near_items = jnp.concatenate([near[j, :pairs, :], near[j + 1, :pairs, :]], axis=0)
            e = exp_of(dot(far_items, q, NT), width)
            total = total + jnp.sum(e.reshape(both // 8, 8, 2 * both), axis=0)
            e = exp_of(dot(near_items, far_q, NT), width)
            far_total = far_total + jnp.sum(e.reshape(both // 8, 8, both), axis=0)
        total = jnp.sum(total, axis=0, keepdims=True)
        far_total = jnp.sum(far_total, axis=0, keepdims=True)
        for u in range(2):
            inverse[y + u] = jnp.concatenate(
                [
                    total[:, u * both : u * both + pairs] + near_sums[y + u],
                    total[:, u * both + pairs : (u + 1) * both] + far_total[:, u * pairs : (u + 1) * pairs],
                ],
                axis=1,
            )
        return carry

    for h in range(chips // 2):
        denominators(h, 0)
    item_own, query_own = near[own, :pairs, :], near[own, pairs:, :]
    own_hits = iota((pairs, pairs), 0) == iota((pairs, pairs), 1)
    diagonal = jnp.sum(
        jnp.where(own_hits, dot(item_own, query_own, NT) * scale, 0.0), axis=0, keepdims=True
    )
    loss_ref[...] = jnp.log(inverse[own][:, :pairs]) - diagonal
    ones = hits(iota((pairs, both), 0), iota((pairs, both), 1))
    grad_item = jnp.zeros((pairs, width), jnp.float32)
    row_total = jnp.zeros((pairs, LANES), jnp.float32)
    for y in range(chips):
        q = queries(y)
        soft = exp_of(dot(item_own, q, NT), width) * (1.0 / inverse[y])
        soft = soft - jnp.where(own == y, ones, 0.0)
        grad_item = grad_item + dot(soft.astype(jnp.bfloat16), q)
        e = exp_of(dot(query_own, items(y), NT), width)
        own_exp[y] = e
        for b in range(both // LANES):
            row_total = row_total + e[:, b * LANES : (b + 1) * LANES]
    row_inverse = 1.0 / jnp.sum(row_total, axis=1, keepdims=True)
    grad_query = jnp.zeros((pairs, width), jnp.float32)
    for y in range(chips):
        soft = own_exp[y] * row_inverse - jnp.where(own == y, ones, 0.0)
        grad_query = grad_query + dot(soft.astype(jnp.bfloat16), items(y))
    backs = []
    for side, grad in enumerate((grad_item, grad_query)):
        span = pl.ds(side * pairs, pairs)
        grad = grad * scale
        normed, factor = project(pool_ref[span, :], weights_ref[side])
        inner_mean = jnp.mean(grad * normed, axis=1, keepdims=True)
        grad_hidden = (factor * (grad - normed * inner_mean)).astype(jnp.bfloat16)
        backs.append(dot(grad_hidden, weights_ref[side], NT))
    back = jnp.concatenate(backs, axis=0)
    high = back.astype(jnp.bfloat16)
    low = (back - high.astype(jnp.float32)).astype(jnp.bfloat16)
    split = jnp.concatenate([high, low], axis=1)
    step = 256
    for weights, out in ((turned_ref, grads_ref), (more_turned_ref, more_grads_ref)):
        for s in range(0, weights.shape[0], step):
            parts = dot(weights[s : s + step, :], split)
            out[s : s + step, :] = (parts[:, :width] + parts[:, width:]).astype(jnp.bfloat16)


def column_body(y_ref, codes_ref, more_codes_ref, grads_ref, more_grads_ref, out_ref, *, side):
    chips, per = out_ref.shape[:2]
    parity = y_ref[0] % 2
    for n in range(0, chips, 2):
        total = None
        for codes, grads in ((codes_ref, grads_ref), (more_codes_ref, more_grads_ref)):
            hot = [
                hits(iota((per, codes.shape[1]), 0), codes[...] - ((n + u) * CORES + side) * per)
                for u in range(2)
            ]
            part = dot(jnp.concatenate(hot, axis=0).astype(jnp.bfloat16), grads[...])
            total = part if total is None else total + part
        for u in range(2):
            half, k = divmod(n + u, chips // 2)
            owner_y = 2 * k + (parity if half == 0 else 1 - parity)
            out_ref[owner_y] = total[u * per : (u + 1) * per].astype(out_ref.dtype)


def add_body(a_ref, b_ref, out_ref):
    out_ref[...] = (a_ref[...] + b_ref[...].astype(jnp.float32)).astype(jnp.bfloat16)


def adagrad_body(parts_ref, table_ref, accum_ref, new_table_ref, new_accum_ref):
    grad = parts_ref[0].astype(jnp.float32)
    for y in range(1, parts_ref.shape[0]):
        grad = grad + parts_ref[y].astype(jnp.float32)
    rows, width = grad.shape
    mean = jnp.sum(grad * grad, axis=1, keepdims=True) * (1.0 / width)
    across = jnp.sum(
        jnp.where(iota((rows, rows), 0) == iota((rows, rows), 1), mean, 0.0), axis=0, keepdims=True
    )
    down = jnp.sum(
        jnp.where(iota((rows, rows), 0) == iota((rows, rows), 1), accum_ref[...], 0.0),
        axis=1,
        keepdims=True,
    )
    new_accum_ref[...] = accum_ref[...] + across
    new_table_ref[...] = table_ref[...] - learn_rate * grad / jnp.sqrt(down + mean)


def on_device(
    table, accum, item_weight, query_weight, packed_rows, block_counts, item_refs, query_refs
):
    bf16, f32, i32 = jnp.bfloat16, jnp.float32, jnp.int32
    shape = jax.ShapeDtypeStruct
    n_dp, n_table = lax.axis_size("dp"), lax.axis_size("table")
    chips = n_dp // CORES
    per, width = table.shape
    pairs = item_refs.shape[2]
    slots = CAP * n_dp
    base = slots * 3 // 4
    more = slots - base
    replica = lax.axis_index("dp")
    core = (replica % CORES).reshape(1).astype(i32)
    chip = (replica // CORES).reshape(1).astype(i32)
    along_y = [[y * CORES + c for y in range(chips)] for c in range(CORES)]
    along_parity = [
        [(2 * k + p) * CORES + c for k in range(chips // 2)] for p in range(2) for c in range(CORES)
    ]
    swap = [(r, r ^ 1) for r in range(n_dp)]
    beside = [
        (y * CORES + c, (y + (chips - 1 if c == 0 else 1)) % chips * CORES + c)
        for y in range(chips)
        for c in range(CORES)
    ]

    def over_y(x):
        return lax.all_to_all(
            x, "dp", split_axis=0, concat_axis=0, axis_index_groups=along_y, tiled=True
        )

    def over_table(x):
        parts = x.reshape(n_table, -1, x.shape[-1])
        return lax.all_to_all(parts, "table", split_axis=0, concat_axis=0, tiled=True).reshape(x.shape)

    own_rows = table.astype(bf16)
    chip_rows = jnp.concatenate([own_rows, lax.ppermute(own_rows, "dp", swap)])
    near_rows = lax.all_to_all(
        jnp.broadcast_to(chip_rows[None], (chips // 2, CORES * per, width)),
        "dp",
        split_axis=0,
        concat_axis=0,
        axis_index_groups=along_parity,
        tiled=True,
    )
    tower_weights = jnp.stack([item_weight, query_weight])
    items, queries = item_refs[0, 0].T, query_refs[0, 0].T
    requests, places, old_accum = call(
        functools.partial(request_body, base=base),
        (shape((n_table, slots + 8), i32), shape((n_table, slots), i32), shape((1, per), f32)),
        [SMEM] * 2 + [VMEM] * 5,
        [
            pltpu.VMEM((32, LANES), f32),
            pltpu.VMEM((n_dp * n_table // LANES, LANES), f32),
            pltpu.VMEM((LANES, LANES), f32),
        ],
    )(chip, core, packed_rows.reshape(1, -1), block_counts.reshape(1, -1), items, queries, accum.reshape(1, per))
    near_rows, requests = lax.optimization_barrier((near_rows, requests))
    next_rows = lax.ppermute(near_rows, "dp", beside)
    received = over_table(requests)

    def pick(first, count, received):
        return call(
            functools.partial(pick_body, first=first, count=count, slots=slots),
            (shape((n_table * count, width), bf16), shape((1,), i32)),
            [VMEM] * 3,
            [pltpu.VMEM((LANES, LANES), f32)],
            out_specs=(VMEM, SMEM),
        )(received, near_rows, next_rows)

    picked, over = pick(0, base, received)
    fetched = over_table(picked)
    crowded = over[0] > 0
    nothing = jnp.zeros((n_table * more, width), bf16)
    late, fetched = lax.optimization_barrier((received, fetched))
    more_fetched = lax.cond(
        crowded, lambda: over_table(pick(base, more, late)[0]), lambda: nothing
    )
    pair_hits, more_hits, pool, spread = call(
        tower_body,
        (
            shape((2 * pairs, n_table * base), bf16),
            shape((2 * pairs, n_table * more), bf16),
            shape((2 * pairs, width), bf16),
            shape((chips, 2 * pairs, width), bf16),
        ),
        [VMEM] * 6 + [pl.BlockSpec(memory_space=pl.ANY), VMEM],
        [
            pltpu.VMEM((LANES, LANES), f32),
            pltpu.VMEM((2 * pairs, width), f32),
            pltpu.VMEM((n_table * more, width), bf16),
            pltpu.SemaphoreType.DMA,
        ],
    )(
        received,
        places[:, :base].reshape(1, -1),
        places[:, base:].reshape(1, -1),
        items,
        queries,
        fetched,
        more_fetched,
        tower_weights,
    )
    near = over_y(spread)
    far = lax.ppermute(near, "dp", swap)
    near_sums, turned_hits, more_turned_hits = call(
        near_body,
        (
            shape((chips, 1, pairs), f32),
            shape((n_table * base, 2 * pairs), bf16),
            shape((n_table * more, 2 * pairs), bf16),
        ),
        [VMEM] * 3,
    )(near, pair_hits, more_hits)
    loss, grads, more_grads = call(
        loss_body,
        (
            shape((1, pairs), f32),
            shape((n_table * base, width), bf16),
            shape((n_table * more, width), bf16),
        ),
        [SMEM] + [VMEM] * 7,
        [pltpu.VMEM((chips, 1, 2 * pairs), f32), pltpu.VMEM((chips, pairs, 2 * pairs), f32)],
    )(chip, near, far, near_sums, pool, tower_weights, turned_hits, more_turned_hits)
    returned = over_table(grads)
    more_returned = lax.cond(crowded, lambda: over_table(more_grads), lambda: nothing)
    codes = received[:, :base].reshape(1, -1)
    more_codes = received[:, base:slots].reshape(1, -1)

    def column(side, dtype):
        return call(
            functools.partial(column_body, side=side),
            shape((chips, per, width), dtype),
            [SMEM] + [VMEM] * 4,
        )(chip, codes, more_codes, returned, more_returned)

    other = lax.ppermute(column(1, bf16), "dp", swap)
    both = call(add_body, shape((chips, per, width), bf16), [VMEM] * 2)(column(0, f32), other)
    new_table, new_accum = call(
        adagrad_body, (shape((per, width), f32), shape((1, per), f32)), [VMEM] * 3
    )(over_y(both), table, old_accum)
    return (new_table, new_accum.reshape(per), loss.reshape(1, 1, pairs))


def solution(mesh):
    in_specs = (
        P(("dp", "table"), None),
        P(("dp", "table")),
        P(),
        P(),
        P("dp", "table", None),
        P("dp", "table", None),
        P("dp", "table", None, None),
        P("dp", "table", None, None),
    )
    out_specs = (P(("dp", "table"), None), P(("dp", "table")), P("dp", "table", None))
    return jax.shard_map(
        on_device, mesh=mesh, in_specs=in_specs, out_specs=out_specs, check_vma=False
    )
```

```python
import functools
import math

import jax
import jax.numpy as jnp
from jax import lax
from jax.experimental import pallas as pl
from jax.experimental.pallas import tpu as pltpu
from jax.sharding import PartitionSpec as P

CAP = 2
LANES = 128
CORES = 2

learn_rate = 0.3
epsilon = 1e-06
sharpness = 3.0

VMEM = pl.BlockSpec(memory_space=pltpu.VMEM)
SMEM = pl.BlockSpec(memory_space=pltpu.SMEM)

NT = (((1,), (1,)), ((), ()))


def iota(shape, axis):
    return lax.broadcasted_iota(jnp.int32, shape, axis)


def dot(a, b, dims=(((1,), (0,)), ((), ()))):
    return lax.dot_general(a, b, dims, preferred_element_type=jnp.float32)


def hits(a, b):
    return jnp.where(a == b, 1.0, 0.0)


def call(body, out_shape, in_specs, scratch=(), out_specs=None):
    return pl.pallas_call(
        body,
        out_shape=out_shape,
        in_specs=in_specs,
        out_specs=jax.tree.map(lambda _: VMEM, out_shape) if out_specs is None else out_specs,
        scratch_shapes=list(scratch),
        compiler_params=pltpu.CompilerParams(vmem_limit_bytes=12 * 1024 * 1024),
    )


def request_body(
    y_ref, core_ref, list_ref, counts_ref, item_refs, query_refs, accum_ref,
    req_ref, pos_ref, accum_out, looked, counts2d, square, *, base,
):
    length, owners = list_ref.shape[1], counts_ref.shape[1]
    rows = owners // LANES
    depth = looked.shape[0] // 2
    groups, slots = pos_ref.shape
    accum_out[...] = accum_ref[...]
    looked[...] = jnp.zeros_like(looked)
    for b in range(length // LANES):
        looked[b : b + 1, :] = list_ref[:, b * LANES : (b + 1) * LANES].astype(jnp.float32)
    for b in range(rows):
        counts2d[b : b + 1, :] = counts_ref[:, b * LANES : (b + 1) * LANES].astype(jnp.float32)
    down = iota((LANES, LANES), 0)
    block = iota((depth, LANES), 0)
    wanted = jnp.zeros((depth, LANES), jnp.float32)
    for refs_ref in (item_refs, query_refs):
        for l in range(refs_ref.shape[0]):
            ref = refs_ref[l : l + 1, :]
            high = hits(block, ref >> 7).astype(jnp.bfloat16)
            low = hits(down, ref & (LANES - 1)).astype(jnp.bfloat16)
            wanted = wanted + dot(high, low, NT)
    looked[depth:, :] = jnp.where(wanted > 0.5, 1.0, 0.0)
    looked_bf = looked[...].astype(jnp.bfloat16)

    counts = counts2d[...]
    counts_bf = counts.astype(jnp.bfloat16)
    before = hits(down < iota((LANES, LANES), 1), True).astype(jnp.bfloat16)
    within = dot(counts_bf, before)
    row_total = dot(counts_bf, jnp.ones((LANES, LANES), jnp.bfloat16))
    offsets = [jnp.zeros((1, LANES), jnp.float32)]
    for i in range(rows - 1):
        offsets.append(offsets[-1] + row_total[i : i + 1, :])
    starts = within + jnp.concatenate(offsets, axis=0)
    second = jnp.where(counts > 1.5, starts + 1.0, -1.0)
    positions = jnp.concatenate([starts, second], axis=0)
    pos_int = positions.astype(jnp.int32)
    entries = CAP * rows
    width = LANES // CORES
    owner_core = jnp.where(iota((1, LANES), 1) < width, 0, 1)
    side = jnp.where(owner_core == core_ref[0], 0.0, 1.0)
    parity = y_ref[0] % 2
    square[...] = jnp.zeros_like(square)
    square[entries : 2 * entries, :] = positions
    for r in range(entries):
        p = pos_int[r : r + 1, :]
        spread = dot(looked_bf, hits(down, p & (LANES - 1)).astype(jnp.bfloat16))
        here = block == (p >> 7)
        value = jnp.sum(jnp.where(here, spread[:depth], 0.0), axis=0, keepdims=True)
        used = jnp.sum(jnp.where(here, spread[depth:], 0.0), axis=0, keepdims=True)
        y = r % rows
        apart = jnp.where(parity == y % 2, 0, rows // 2).astype(jnp.float32)
        square[r : r + 1, :] = value + (side * rows + apart + y // 2) * LANES
        square[2 * entries + r : 2 * entries + r + 1, :] = used
    turned = square[...].T

    def column(n):
        part = slice(n * entries, (n + 1) * entries)
        return jnp.concatenate([turned[:width, part], turned[width:, part]], axis=1)

    codes, places, used = column(0), column(1), column(2)
    before = hits(iota((slots, slots), 0) < iota((slots, slots), 1), True).astype(jnp.bfloat16)
    rank = dot(used.astype(jnp.bfloat16), before)
    rank = jnp.where(used > 0.5, rank, -1.0).astype(jnp.int32)
    slot = iota((groups, slots), 1)
    packed_codes = jnp.full((groups, slots), -1.0, jnp.float32)
    packed_places = packed_codes
    for k in range(slots):
        here = slot == rank[:, k : k + 1]
        packed_codes = jnp.where(here, codes[:, k : k + 1], packed_codes)
        packed_places = jnp.where(here, places[:, k : k + 1], packed_places)
    over = jnp.max(rank, axis=1, keepdims=True)
    over = jnp.max(over, axis=0, keepdims=True)
    over = jnp.where(over >= base, 1, 0)
    pos_ref[...] = packed_places.astype(jnp.int32)
    req_ref[:, :slots] = packed_codes.astype(jnp.int32)
    req_ref[:, slots:] = jnp.broadcast_to(over, (groups, req_ref.shape[1] - slots))


def pick_rows(turned_ref, row_refs, out_ref, first, count, begin):
    groups = out_ref.shape[0] // count
    rows = jnp.concatenate([ref[...].reshape(-1, ref.shape[-1]) for ref in row_refs], axis=0)
    lane = iota((count, LANES), 1)
    step = 8
    for t in range(0, groups, step):
        hot = []
        for u in range(t, t + step):
            code = jnp.broadcast_to(turned_ref[first : first + count, u : u + 1], (count, LANES))
            hot.append(
                jnp.concatenate(
                    [hits(lane + (begin + b * LANES), code) for b in range(rows.shape[0] // LANES)],
                    axis=1,
                )
            )
        hot = jnp.concatenate(hot, axis=0).astype(jnp.bfloat16)
        yield pl.ds(t * count, step * count), dot(hot, rows)


def pick_near_body(recv_ref, near_ref, next_ref, out_ref, turned_ref, over_ref, square, *, first, count, slots):
    groups = recv_ref.shape[0]
    square[...] = jnp.zeros_like(square)
    square[:groups, : recv_ref.shape[1]] = recv_ref[...].astype(jnp.float32)
    turned_ref[...] = square[...].T.astype(jnp.int32)
    over_ref[0] = jnp.max(turned_ref[slots : slots + 1, :groups])
    for span, got in pick_rows(turned_ref, (near_ref, next_ref), out_ref, first, count, 0):
        out_ref[span, :] = got.astype(jnp.bfloat16)


def pick_far_body(turned_ref, far_ref, near_got, out_ref, *, first, count):
    begin = far_ref.shape[0] * far_ref.shape[1]
    for span, got in pick_rows(turned_ref, (far_ref,), out_ref, first, count, begin):
        out_ref[span, :] = (got + near_got[span, :].astype(jnp.float32)).astype(jnp.bfloat16)


def project(pool, weight):
    hidden = dot(pool, weight)
    factor = lax.rsqrt(jnp.mean(hidden * hidden, axis=1, keepdims=True) + epsilon)
    return hidden * factor, factor


def pair_weight(refs, pos):
    weight = hits(refs[:, 0:1], pos)
    for l in range(1, refs.shape[1]):
        weight = weight + hits(refs[:, l : l + 1], pos)
    return weight.astype(jnp.bfloat16)


def tower_body(
    recv_ref, pos_ref, more_pos_ref, item_refs, query_refs, fetched, more_fetched, weights,
    hits_ref, more_hits_ref, pool_ref, out_ref, square, pool_sum, more_rows, sem,
):
    pairs = item_refs.shape[1]
    square[...] = jnp.zeros_like(square)
    square[0 : item_refs.shape[0], :] = item_refs[...].astype(jnp.float32)
    square[8 : 8 + query_refs.shape[0], :] = query_refs[...].astype(jnp.float32)
    turned = square[...].T.astype(jnp.int32)
    item_columns = turned[:, 0 : item_refs.shape[0]]
    query_columns = turned[:, 8 : 8 + query_refs.shape[0]]
    slots = (pos_ref.shape[1] + more_pos_ref.shape[1]) // recv_ref.shape[0]
    crowded = jnp.max(recv_ref[:, slots : slots + 1]) > 0
    spans = [pl.ds(side * pairs, pairs) for side in range(2)]
    for span, refs in zip(spans, (item_columns, query_columns)):
        weight = pair_weight(refs, pos_ref[...])
        hits_ref[span, :] = weight
        pool_sum[span, :] = dot(weight, fetched[...])
    more_hits_ref[...] = jnp.zeros_like(more_hits_ref)

    @pl.when(crowded)
    def _():
        copy = pltpu.make_async_copy(more_fetched, more_rows, sem)
        copy.start()
        copy.wait()
        for span, refs in zip(spans, (item_columns, query_columns)):
            weight = pair_weight(refs, more_pos_ref[...])
            more_hits_ref[span, :] = weight
            pool_sum[span, :] = pool_sum[span, :] + dot(weight, more_rows[...])

    outs = []
    for side, span in enumerate(spans):
        pool = pool_sum[span, :].astype(jnp.bfloat16)
        pool_ref[span, :] = pool
        outs.append(project(pool, weights[side])[0].astype(jnp.bfloat16))
    for y in range(out_ref.shape[0]):
        out_ref[y, :pairs, :] = outs[0]
        out_ref[y, pairs:, :] = outs[1]


def scale_of(width):
    return sharpness * width ** (-0.5)


def exp_of(products, width):
    return jnp.exp2(products * (scale_of(width) * math.log2(math.e)))


def near_body(
    near, pool_ref, weights_ref, hits_ref, more_hits_ref,
    sums_ref, normed_ref, factor_ref, turned_ref, more_turned_ref,
):
    chips, both, width = near.shape
    pairs = both // 2
    step = 256
    for weights, out in ((hits_ref, turned_ref), (more_hits_ref, more_turned_ref)):
        for s in range(0, weights.shape[1], step):
            out[s : s + step, :] = weights[:, s : s + step].T
    for side in range(2):
        span = pl.ds(side * pairs, pairs)
        normed, factor = project(pool_ref[span, :], weights_ref[side])
        normed_ref[span, :] = normed
        factor_ref[span, :] = jnp.broadcast_to(factor, (pairs, LANES))
    for y in range(0, chips, 2):
        q = jnp.concatenate([near[y, pairs:, :], near[y + 1, pairs:, :]], axis=0)
        total = jnp.zeros((8, both), jnp.float32)
        for j in range(0, chips, 2):
            items = jnp.concatenate([near[j, :pairs, :], near[j + 1, :pairs, :]], axis=0)
            e = exp_of(dot(items, q, NT), width)
            total = total + jnp.sum(e.reshape(both // 8, 8, both), axis=0)
        total = jnp.sum(total, axis=0, keepdims=True)
        sums_ref[y] = total[:, :pairs]
        sums_ref[y + 1] = total[:, pairs:]


def loss_body(
    y_ref, near, far, near_sums, normed_ref, factor_ref, weights_ref, turned_ref, more_turned_ref,
    loss_ref, grads_ref, more_grads_ref, inverse, own_exp,
):
    chips, both, width = near.shape
    pairs = both // 2
    scale = scale_of(width)
    own = y_ref[0]

    def items(y):
        return jnp.concatenate([near[y, :pairs, :], far[y, :pairs, :]], axis=0)

    def queries(y):
        return jnp.concatenate([near[y, pairs:, :], far[y, pairs:, :]], axis=0)

    def denominators(h, carry):
        y = 2 * h
        q = jnp.concatenate([queries(y), queries(y + 1)], axis=0)
        far_q = jnp.concatenate([far[y, pairs:, :], far[y + 1, pairs:, :]], axis=0)
        total = jnp.zeros((8, 2 * both), jnp.float32)
        far_total = jnp.zeros((8, both), jnp.float32)
        for j in range(0, chips, 2):
            far_items = jnp.concatenate([far[j, :pairs, :], far[j + 1, :pairs, :]], axis=0)
            near_items = jnp.concatenate([near[j, :pairs, :], near[j + 1, :pairs, :]], axis=0)
            e = exp_of(dot(far_items, q, NT), width)
            total = total + jnp.sum(e.reshape(both // 8, 8, 2 * both), axis=0)
            e = exp_of(dot(near_items, far_q, NT), width)
            far_total = far_total + jnp.sum(e.reshape(both // 8, 8, both), axis=0)
        total = jnp.sum(total, axis=0, keepdims=True)
        far_total = jnp.sum(far_total, axis=0, keepdims=True)
        for u in range(2):
            inverse[y + u] = jnp.concatenate(
                [
                    total[:, u * both : u * both + pairs] + near_sums[y + u],
                    total[:, u * both + pairs : (u + 1) * both] + far_total[:, u * pairs : (u + 1) * pairs],
                ],
                axis=1,
            )
        return carry

    for h in range(chips // 2):
        denominators(h, 0)
    item_own, query_own = near[own, :pairs, :], near[own, pairs:, :]
    own_hits = iota((pairs, pairs), 0) == iota((pairs, pairs), 1)
    diagonal = jnp.sum(
        jnp.where(own_hits, dot(item_own, query_own, NT) * scale, 0.0), axis=0, keepdims=True
    )
    loss_ref[...] = jnp.log(inverse[own][:, :pairs]) - diagonal
    ones = hits(iota((pairs, both), 0), iota((pairs, both), 1))
    grad_item = jnp.zeros((pairs, width), jnp.float32)
    row_total = jnp.zeros((pairs, LANES), jnp.float32)
    for y in range(chips):
        q = queries(y)
        soft = exp_of(dot(item_own, q, NT), width) * (1.0 / inverse[y])
        soft = soft - jnp.where(own == y, ones, 0.0)
        grad_item = grad_item + dot(soft.astype(jnp.bfloat16), q)
        e = exp_of(dot(query_own, items(y), NT), width)
        own_exp[y] = e
        for b in range(both // LANES):
            row_total = row_total + e[:, b * LANES : (b + 1) * LANES]
    row_inverse = 1.0 / jnp.sum(row_total, axis=1, keepdims=True)
    grad_query = jnp.zeros((pairs, width), jnp.float32)
    for y in range(chips):
        soft = own_exp[y] * row_inverse - jnp.where(own == y, ones, 0.0)
        grad_query = grad_query + dot(soft.astype(jnp.bfloat16), items(y))
    backs = []
    for side, grad in enumerate((grad_item, grad_query)):
        span = pl.ds(side * pairs, pairs)
        grad = grad * scale
        normed, factor = normed_ref[span, :], factor_ref[span, 0:1]
        inner_mean = jnp.mean(grad * normed, axis=1, keepdims=True)
        grad_hidden = (factor * (grad - normed * inner_mean)).astype(jnp.bfloat16)
        backs.append(dot(grad_hidden, weights_ref[side], NT))
    back = jnp.concatenate(backs, axis=0).astype(jnp.bfloat16)
    for weights, out in ((turned_ref, grads_ref), (more_turned_ref, more_grads_ref)):
        out[...] = dot(weights[...], back).astype(jnp.bfloat16)


def column_body(y_ref, codes_ref, more_codes_ref, grads_ref, more_grads_ref, out_ref, *, side):
    chips, per = out_ref.shape[:2]
    parity = y_ref[0] % 2
    for n in range(0, chips, 2):
        begin = (side * chips + n) * per
        total = None
        for codes, grads in ((codes_ref, grads_ref), (more_codes_ref, more_grads_ref)):
            down = iota((2 * per, codes.shape[1]), 0)
            hot = hits(down, codes[...] - begin).astype(jnp.bfloat16)
            part = dot(hot, grads[...])
            total = part if total is None else total + part
        for u in range(2):
            half, k = divmod(n + u, chips // 2)
            owner_y = 2 * k + (parity if half == 0 else 1 - parity)
            out_ref[owner_y] = total[u * per : (u + 1) * per].astype(out_ref.dtype)


def add_body(a_ref, b_ref, out_ref):
    out_ref[...] = (a_ref[...] + b_ref[...].astype(jnp.float32)).astype(jnp.bfloat16)


def adagrad_body(parts_ref, table_ref, accum_ref, new_table_ref, new_accum_ref):
    grad = parts_ref[0].astype(jnp.float32)
    for y in range(1, parts_ref.shape[0]):
        grad = grad + parts_ref[y].astype(jnp.float32)
    rows, width = grad.shape
    mean = jnp.sum(grad * grad, axis=1, keepdims=True) * (1.0 / width)
    across = jnp.sum(
        jnp.where(iota((rows, rows), 0) == iota((rows, rows), 1), mean, 0.0), axis=0, keepdims=True
    )
    down = jnp.sum(
        jnp.where(iota((rows, rows), 0) == iota((rows, rows), 1), accum_ref[...], 0.0),
        axis=1,
        keepdims=True,
    )
    new_accum_ref[...] = accum_ref[...] + across
    new_table_ref[...] = table_ref[...] - learn_rate * grad / jnp.sqrt(down + mean)


def on_device(
    table, accum, item_weight, query_weight, packed_rows, block_counts, item_refs, query_refs
):
    bf16, f32, i32 = jnp.bfloat16, jnp.float32, jnp.int32
    shape = jax.ShapeDtypeStruct
    n_dp, n_table = lax.axis_size("dp"), lax.axis_size("table")
    chips = n_dp // CORES
    per, width = table.shape
    pairs = item_refs.shape[2]
    slots = CAP * n_dp
    base = slots * 3 // 4
    more = slots - base
    replica = lax.axis_index("dp")
    core = (replica % CORES).reshape(1).astype(i32)
    chip = (replica // CORES).reshape(1).astype(i32)
    along_y = [[y * CORES + c for y in range(chips)] for c in range(CORES)]
    along_parity = [
        [(2 * k + p) * CORES + c for k in range(chips // 2)] for p in range(2) for c in range(CORES)
    ]
    swap = [(r, r ^ 1) for r in range(n_dp)]
    beside = [
        (y * CORES + c, (y + (chips - 1 if c == 0 else 1)) % chips * CORES + c)
        for y in range(chips)
        for c in range(CORES)
    ]

    def over_y(x):
        return lax.all_to_all(
            x, "dp", split_axis=0, concat_axis=0, axis_index_groups=along_y, tiled=True
        )

    def over_table(x):
        parts = x.reshape(n_table, -1, x.shape[-1])
        return lax.all_to_all(parts, "table", split_axis=0, concat_axis=0, tiled=True).reshape(x.shape)

    near_rows = lax.all_to_all(
        jnp.broadcast_to(table.astype(bf16)[None], (chips // 2, per, width)),
        "dp",
        split_axis=0,
        concat_axis=0,
        axis_index_groups=along_parity,
        tiled=True,
    )
    tower_weights = jnp.stack([item_weight, query_weight])
    items, queries = item_refs[0, 0].T, query_refs[0, 0].T
    requests, places, old_accum = call(
        functools.partial(request_body, base=base),
        (shape((n_table, slots + 8), i32), shape((n_table, slots), i32), shape((1, per), f32)),
        [SMEM] * 2 + [VMEM] * 5,
        [
            pltpu.VMEM((32, LANES), f32),
            pltpu.VMEM((n_dp * n_table // LANES, LANES), f32),
            pltpu.VMEM((LANES, LANES), f32),
        ],
    )(chip, core, packed_rows.reshape(1, -1), block_counts.reshape(1, -1), items, queries, accum.reshape(1, per))
    near_rows, requests = lax.optimization_barrier((near_rows, requests))
    next_rows = lax.ppermute(near_rows, "dp", beside)
    received = over_table(requests)
    received, near_rows, next_rows = lax.optimization_barrier((received, near_rows, next_rows))
    far_rows = lax.ppermute(jnp.concatenate([near_rows, next_rows]), "dp", swap)

    def pick(first, count, received):
        picked = shape((n_table * count, width), bf16)
        near_got, turned, over = call(
            functools.partial(pick_near_body, first=first, count=count, slots=slots),
            (picked, shape((LANES, LANES), i32), shape((1,), i32)),
            [VMEM] * 3,
            [pltpu.VMEM((LANES, LANES), f32)],
            out_specs=(VMEM, VMEM, SMEM),
        )(received, near_rows, next_rows)
        return call(
            functools.partial(pick_far_body, first=first, count=count), picked, [VMEM] * 3
        )(turned, far_rows, near_got), over

    picked, over = pick(0, base, received)
    fetched = over_table(picked)
    crowded = over[0] > 0
    nothing = jnp.zeros((n_table * more, width), bf16)
    late, fetched = lax.optimization_barrier((received, fetched))
    more_fetched = lax.cond(
        crowded, lambda: over_table(pick(base, more, late)[0]), lambda: nothing
    )
    pair_hits, more_hits, pool, spread = call(
        tower_body,
        (
            shape((2 * pairs, n_table * base), bf16),
            shape((2 * pairs, n_table * more), bf16),
            shape((2 * pairs, width), bf16),
            shape((chips, 2 * pairs, width), bf16),
        ),
        [VMEM] * 6 + [pl.BlockSpec(memory_space=pl.ANY), VMEM],
        [
            pltpu.VMEM((LANES, LANES), f32),
            pltpu.VMEM((2 * pairs, width), f32),
            pltpu.VMEM((n_table * more, width), bf16),
            pltpu.SemaphoreType.DMA,
        ],
    )(
        received,
        places[:, :base].reshape(1, -1),
        places[:, base:].reshape(1, -1),
        items,
        queries,
        fetched,
        more_fetched,
        tower_weights,
    )
    near = over_y(spread)
    far = lax.ppermute(near, "dp", swap)
    near_sums, normed, factor, turned_hits, more_turned_hits = call(
        near_body,
        (
            shape((chips, 1, pairs), f32),
            shape((2 * pairs, width), f32),
            shape((2 * pairs, LANES), f32),
            shape((n_table * base, 2 * pairs), bf16),
            shape((n_table * more, 2 * pairs), bf16),
        ),
        [VMEM] * 5,
    )(near, pool, tower_weights, pair_hits, more_hits)
    loss, grads, more_grads = call(
        loss_body,
        (
            shape((1, pairs), f32),
            shape((n_table * base, width), bf16),
            shape((n_table * more, width), bf16),
        ),
        [SMEM] + [VMEM] * 8,
        [pltpu.VMEM((chips, 1, 2 * pairs), f32), pltpu.VMEM((chips, pairs, 2 * pairs), f32)],
    )(chip, near, far, near_sums, normed, factor, tower_weights, turned_hits, more_turned_hits)
    returned = over_table(grads)
    more_returned = lax.cond(crowded, lambda: over_table(more_grads), lambda: nothing)
    codes = received[:, :base].reshape(1, -1)
    more_codes = received[:, base:slots].reshape(1, -1)

    def column(side, dtype):
        return call(
            functools.partial(column_body, side=side),
            shape((chips, per, width), dtype),
            [SMEM] + [VMEM] * 4,
        )(chip, codes, more_codes, returned, more_returned)

    other = lax.ppermute(column(1, bf16), "dp", swap)
    both = call(add_body, shape((chips, per, width), bf16), [VMEM] * 2)(column(0, f32), other)
    new_table, new_accum = call(
        adagrad_body, (shape((per, width), f32), shape((1, per), f32)), [VMEM] * 3
    )(over_y(both), table, old_accum)
    return (new_table, new_accum.reshape(per), loss.reshape(1, 1, pairs))


def solution(mesh):
    in_specs = (
        P(("dp", "table"), None),
        P(("dp", "table")),
        P(),
        P(),
        P("dp", "table", None),
        P("dp", "table", None),
        P("dp", "table", None, None),
        P("dp", "table", None, None),
    )
    out_specs = (P(("dp", "table"), None), P(("dp", "table")), P("dp", "table", None))
    return jax.shard_map(
        on_device, mesh=mesh, in_specs=in_specs, out_specs=out_specs, check_vma=False
    )
```

```python
import functools
import math

import jax
import jax.numpy as jnp
from jax import lax
from jax.experimental import pallas as pl
from jax.experimental.pallas import tpu as pltpu
from jax.sharding import PartitionSpec as P

CAP = 2
LANES = 128
CORES = 2

learn_rate = 0.3
epsilon = 1e-06
sharpness = 3.0

VMEM = pl.BlockSpec(memory_space=pltpu.VMEM)
SMEM = pl.BlockSpec(memory_space=pltpu.SMEM)

NT = (((1,), (1,)), ((), ()))


def iota(shape, axis):
    return lax.broadcasted_iota(jnp.int32, shape, axis)


def dot(a, b, dims=(((1,), (0,)), ((), ()))):
    return lax.dot_general(a, b, dims, preferred_element_type=jnp.float32)


def hits(a, b):
    return jnp.where(a == b, 1.0, 0.0)


def call(body, out_shape, in_specs, scratch=(), out_specs=None):
    return pl.pallas_call(
        body,
        out_shape=out_shape,
        in_specs=in_specs,
        out_specs=jax.tree.map(lambda _: VMEM, out_shape) if out_specs is None else out_specs,
        scratch_shapes=list(scratch),
        compiler_params=pltpu.CompilerParams(vmem_limit_bytes=12 * 1024 * 1024),
    )


def request_body(
    y_ref, core_ref, list_ref, counts_ref, item_refs, query_refs, accum_ref,
    req_ref, pos_ref, accum_out, looked, counts2d, square, *, base,
):
    length, owners = list_ref.shape[1], counts_ref.shape[1]
    rows = owners // LANES
    depth = looked.shape[0] // 2
    groups, slots = pos_ref.shape
    accum_out[...] = accum_ref[...]
    looked[...] = jnp.zeros_like(looked)
    for b in range(length // LANES):
        looked[b : b + 1, :] = list_ref[:, b * LANES : (b + 1) * LANES].astype(jnp.float32)
    for b in range(rows):
        counts2d[b : b + 1, :] = counts_ref[:, b * LANES : (b + 1) * LANES].astype(jnp.float32)
    down = iota((LANES, LANES), 0)
    block = iota((depth, LANES), 0)
    wanted = jnp.zeros((depth, LANES), jnp.float32)
    for refs_ref in (item_refs, query_refs):
        for l in range(refs_ref.shape[0]):
            ref = refs_ref[l : l + 1, :]
            high = hits(block, ref >> 7).astype(jnp.bfloat16)
            low = hits(down, ref & (LANES - 1)).astype(jnp.bfloat16)
            wanted = wanted + dot(high, low, NT)
    looked[depth:, :] = jnp.where(wanted > 0.5, 1.0, 0.0)
    looked_bf = looked[...].astype(jnp.bfloat16)

    counts = counts2d[...]
    counts_bf = counts.astype(jnp.bfloat16)
    before = hits(down < iota((LANES, LANES), 1), True).astype(jnp.bfloat16)
    within = dot(counts_bf, before)
    row_total = dot(counts_bf, jnp.ones((LANES, LANES), jnp.bfloat16))
    offsets = [jnp.zeros((1, LANES), jnp.float32)]
    for i in range(rows - 1):
        offsets.append(offsets[-1] + row_total[i : i + 1, :])
    starts = within + jnp.concatenate(offsets, axis=0)
    second = jnp.where(counts > 1.5, starts + 1.0, -1.0)
    positions = jnp.concatenate([starts, second], axis=0)
    pos_int = positions.astype(jnp.int32)
    entries = CAP * rows
    width = LANES // CORES
    owner_core = jnp.where(iota((1, LANES), 1) < width, 0, 1)
    side = jnp.where(owner_core == core_ref[0], 0.0, 1.0)
    parity = y_ref[0] % 2
    square[...] = jnp.zeros_like(square)
    square[entries : 2 * entries, :] = positions
    for r in range(entries):
        p = pos_int[r : r + 1, :]
        spread = dot(looked_bf, hits(down, p & (LANES - 1)).astype(jnp.bfloat16))
        here = block == (p >> 7)
        value = jnp.sum(jnp.where(here, spread[:depth], 0.0), axis=0, keepdims=True)
        used = jnp.sum(jnp.where(here, spread[depth:], 0.0), axis=0, keepdims=True)
        y = r % rows
        apart = jnp.where(parity == y % 2, 0, rows // 2).astype(jnp.float32)
        square[r : r + 1, :] = value + (side * rows + apart + y // 2) * LANES
        square[2 * entries + r : 2 * entries + r + 1, :] = used
    turned = square[...].T

    def column(n):
        part = slice(n * entries, (n + 1) * entries)
        return jnp.concatenate([turned[:width, part], turned[width:, part]], axis=1)

    codes, places, used = column(0), column(1), column(2)
    before = hits(iota((slots, slots), 0) < iota((slots, slots), 1), True).astype(jnp.bfloat16)
    rank = dot(used.astype(jnp.bfloat16), before)
    rank = jnp.where(used > 0.5, rank, -1.0).astype(jnp.int32)
    slot = iota((groups, slots), 1)
    packed_codes = jnp.full((groups, slots), -1.0, jnp.float32)
    packed_places = packed_codes
    for k in range(slots):
        here = slot == rank[:, k : k + 1]
        packed_codes = jnp.where(here, codes[:, k : k + 1], packed_codes)
        packed_places = jnp.where(here, places[:, k : k + 1], packed_places)
    over = jnp.max(rank, axis=1, keepdims=True)
    over = jnp.max(over, axis=0, keepdims=True)
    over = jnp.where(over >= base, 1, 0)
    pos_ref[...] = packed_places.astype(jnp.int32)
    req_ref[:, :slots] = packed_codes.astype(jnp.int32)
    req_ref[:, slots:] = jnp.broadcast_to(over, (groups, req_ref.shape[1] - slots))


def pick_rows(turned_ref, row_refs, out_ref, first, count, begin):
    groups = out_ref.shape[0] // count
    rows = jnp.concatenate([ref[...].reshape(-1, ref.shape[-1]) for ref in row_refs], axis=0)
    lane = iota((count, LANES), 1)
    step = 8
    for t in range(0, groups, step):
        hot = []
        for u in range(t, t + step):
            code = jnp.broadcast_to(turned_ref[first : first + count, u : u + 1], (count, LANES))
            hot.append(
                jnp.concatenate(
                    [hits(lane + (begin + b * LANES), code) for b in range(rows.shape[0] // LANES)],
                    axis=1,
                )
            )
        hot = jnp.concatenate(hot, axis=0).astype(jnp.bfloat16)
        yield pl.ds(t * count, step * count), dot(hot, rows)


def pick_near_body(recv_ref, near_ref, next_ref, out_ref, turned_ref, over_ref, square, *, first, count, slots):
    groups = recv_ref.shape[0]
    square[...] = jnp.zeros_like(square)
    square[:groups, : recv_ref.shape[1]] = recv_ref[...].astype(jnp.float32)
    turned_ref[...] = square[...].T.astype(jnp.int32)
    over_ref[0] = jnp.max(turned_ref[slots : slots + 1, :groups])
    for span, got in pick_rows(turned_ref, (near_ref, next_ref), out_ref, first, count, 0):
        out_ref[span, :] = got.astype(jnp.bfloat16)


def pick_far_body(turned_ref, far_ref, near_got, out_ref, *, first, count):
    begin = far_ref.shape[0] * far_ref.shape[1]
    for span, got in pick_rows(turned_ref, (far_ref,), out_ref, first, count, begin):
        out_ref[span, :] = (got + near_got[span, :].astype(jnp.float32)).astype(jnp.bfloat16)


def project(pool, weight):
    hidden = dot(pool, weight)
    factor = lax.rsqrt(jnp.mean(hidden * hidden, axis=1, keepdims=True) + epsilon)
    return hidden * factor, factor


def pair_weight(refs, pos):
    weight = hits(refs[:, 0:1], pos)
    for l in range(1, refs.shape[1]):
        weight = weight + hits(refs[:, l : l + 1], pos)
    return weight.astype(jnp.bfloat16)


def tower_body(
    recv_ref, pos_ref, more_pos_ref, item_refs, query_refs, fetched, more_fetched, weights,
    hits_ref, more_hits_ref, pool_ref, out_ref, square, pool_sum, more_rows, sem,
):
    pairs = item_refs.shape[1]
    square[...] = jnp.zeros_like(square)
    square[0 : item_refs.shape[0], :] = item_refs[...].astype(jnp.float32)
    square[8 : 8 + query_refs.shape[0], :] = query_refs[...].astype(jnp.float32)
    turned = square[...].T.astype(jnp.int32)
    item_columns = turned[:, 0 : item_refs.shape[0]]
    query_columns = turned[:, 8 : 8 + query_refs.shape[0]]
    slots = (pos_ref.shape[1] + more_pos_ref.shape[1]) // recv_ref.shape[0]
    crowded = jnp.max(recv_ref[:, slots : slots + 1]) > 0
    spans = [pl.ds(side * pairs, pairs) for side in range(2)]
    for span, refs in zip(spans, (item_columns, query_columns)):
        weight = pair_weight(refs, pos_ref[...])
        hits_ref[span, :] = weight
        pool_sum[span, :] = dot(weight, fetched[...])
    more_hits_ref[...] = jnp.zeros_like(more_hits_ref)

    @pl.when(crowded)
    def _():
        copy = pltpu.make_async_copy(more_fetched, more_rows, sem)
        copy.start()
        copy.wait()
        for span, refs in zip(spans, (item_columns, query_columns)):
            weight = pair_weight(refs, more_pos_ref[...])
            more_hits_ref[span, :] = weight
            pool_sum[span, :] = pool_sum[span, :] + dot(weight, more_rows[...])

    outs = []
    for side, span in enumerate(spans):
        pool = pool_sum[span, :].astype(jnp.bfloat16)
        pool_ref[span, :] = pool
        outs.append(project(pool, weights[side])[0].astype(jnp.bfloat16))
    for y in range(out_ref.shape[0]):
        out_ref[y, :pairs, :] = outs[0]
        out_ref[y, pairs:, :] = outs[1]


def scale_of(width):
    return sharpness * width ** (-0.5)


def exp_of(products, width):
    return jnp.exp2(products * (scale_of(width) * math.log2(math.e)))


def near_body(
    near, pool_ref, weights_ref, hits_ref, more_hits_ref,
    sums_ref, normed_ref, factor_ref, turned_ref, more_turned_ref,
):
    chips, both, width = near.shape
    pairs = both // 2
    step = 256
    for weights, out in ((hits_ref, turned_ref), (more_hits_ref, more_turned_ref)):
        for s in range(0, weights.shape[1], step):
            out[s : s + step, :] = weights[:, s : s + step].T
    for side in range(2):
        span = pl.ds(side * pairs, pairs)
        normed, factor = project(pool_ref[span, :], weights_ref[side])
        normed_ref[span, :] = normed
        factor_ref[span, :] = jnp.broadcast_to(factor, (pairs, LANES))
    for y in range(0, chips, 2):
        q = jnp.concatenate([near[y, pairs:, :], near[y + 1, pairs:, :]], axis=0)
        total = jnp.zeros((8, both), jnp.float32)
        for j in range(0, chips, 2):
            items = jnp.concatenate([near[j, :pairs, :], near[j + 1, :pairs, :]], axis=0)
            e = exp_of(dot(items, q, NT), width)
            total = total + jnp.sum(e.reshape(both // 8, 8, both), axis=0)
        total = jnp.sum(total, axis=0, keepdims=True)
        sums_ref[y] = total[:, :pairs]
        sums_ref[y + 1] = total[:, pairs:]


def loss_body(
    y_ref, near, far, near_sums, normed_ref, factor_ref, weights_ref, turned_ref, more_turned_ref,
    loss_ref, grads_ref, more_grads_ref, inverse, own_exp,
):
    chips, both, width = near.shape
    pairs = both // 2
    scale = scale_of(width)
    own = y_ref[0]

    def items(y):
        return jnp.concatenate([near[y, :pairs, :], far[y, :pairs, :]], axis=0)

    def queries(y):
        return jnp.concatenate([near[y, pairs:, :], far[y, pairs:, :]], axis=0)

    def denominators(h, carry):
        y = 2 * h
        q = jnp.concatenate([queries(y), queries(y + 1)], axis=0)
        far_q = jnp.concatenate([far[y, pairs:, :], far[y + 1, pairs:, :]], axis=0)
        total = jnp.zeros((8, 2 * both), jnp.float32)
        far_total = jnp.zeros((8, both), jnp.float32)
        for j in range(0, chips, 2):
            far_items = jnp.concatenate([far[j, :pairs, :], far[j + 1, :pairs, :]], axis=0)
            near_items = jnp.concatenate([near[j, :pairs, :], near[j + 1, :pairs, :]], axis=0)
            e = exp_of(dot(far_items, q, NT), width)
            total = total + jnp.sum(e.reshape(both // 8, 8, 2 * both), axis=0)
            e = exp_of(dot(near_items, far_q, NT), width)
            far_total = far_total + jnp.sum(e.reshape(both // 8, 8, both), axis=0)
        total = jnp.sum(total, axis=0, keepdims=True)
        far_total = jnp.sum(far_total, axis=0, keepdims=True)
        for u in range(2):
            inverse[y + u] = jnp.concatenate(
                [
                    total[:, u * both : u * both + pairs] + near_sums[y + u],
                    total[:, u * both + pairs : (u + 1) * both] + far_total[:, u * pairs : (u + 1) * pairs],
                ],
                axis=1,
            )
        return carry

    for h in range(chips // 2):
        denominators(h, 0)
    item_own, query_own = near[own, :pairs, :], near[own, pairs:, :]
    own_hits = iota((pairs, pairs), 0) == iota((pairs, pairs), 1)
    diagonal = jnp.sum(
        jnp.where(own_hits, dot(item_own, query_own, NT) * scale, 0.0), axis=0, keepdims=True
    )
    loss_ref[...] = jnp.log(inverse[own][:, :pairs]) - diagonal
    ones = hits(iota((pairs, both), 0), iota((pairs, both), 1))
    grad_item = jnp.zeros((pairs, width), jnp.float32)
    row_total = jnp.zeros((pairs, LANES), jnp.float32)
    for y in range(chips):
        q = queries(y)
        soft = exp_of(dot(item_own, q, NT), width) * (1.0 / inverse[y])
        soft = soft - jnp.where(own == y, ones, 0.0)
        grad_item = grad_item + dot(soft.astype(jnp.bfloat16), q)
        e = exp_of(dot(query_own, items(y), NT), width)
        own_exp[y] = e
        for b in range(both // LANES):
            row_total = row_total + e[:, b * LANES : (b + 1) * LANES]
    row_inverse = 1.0 / jnp.sum(row_total, axis=1, keepdims=True)
    grad_query = jnp.zeros((pairs, width), jnp.float32)
    for y in range(chips):
        soft = own_exp[y] * row_inverse - jnp.where(own == y, ones, 0.0)
        grad_query = grad_query + dot(soft.astype(jnp.bfloat16), items(y))
    backs = []
    for side, grad in enumerate((grad_item, grad_query)):
        span = pl.ds(side * pairs, pairs)
        grad = grad * scale
        normed, factor = normed_ref[span, :], factor_ref[span, 0:1]
        inner_mean = jnp.mean(grad * normed, axis=1, keepdims=True)
        grad_hidden = (factor * (grad - normed * inner_mean)).astype(jnp.bfloat16)
        backs.append(dot(grad_hidden, weights_ref[side], NT))
    back = jnp.concatenate(backs, axis=0).astype(jnp.bfloat16)
    for weights, out in ((turned_ref, grads_ref), (more_turned_ref, more_grads_ref)):
        out[...] = dot(weights[...], back).astype(jnp.bfloat16)


def column_body(y_ref, codes_ref, more_codes_ref, grads_ref, more_grads_ref, out_ref, *, side):
    chips, per = out_ref.shape[:2]
    parity = y_ref[0] % 2
    for n in range(0, chips, 2):
        begin = (side * chips + n) * per
        total = None
        for codes, grads in ((codes_ref, grads_ref), (more_codes_ref, more_grads_ref)):
            down = iota((2 * per, codes.shape[1]), 0)
            hot = hits(down, codes[...] - begin).astype(jnp.bfloat16)
            part = dot(hot, grads[...])
            total = part if total is None else total + part
        for u in range(2):
            half, k = divmod(n + u, chips // 2)
            owner_y = 2 * k + (parity if half == 0 else 1 - parity)
            out_ref[owner_y] = total[u * per : (u + 1) * per].astype(out_ref.dtype)


def add_body(a_ref, b_ref, out_ref):
    out_ref[...] = (a_ref[...] + b_ref[...].astype(jnp.float32)).astype(jnp.bfloat16)


def adagrad_body(parts_ref, table_ref, accum_ref, new_table_ref, new_accum_ref):
    grad = parts_ref[0].astype(jnp.float32)
    for y in range(1, parts_ref.shape[0]):
        grad = grad + parts_ref[y].astype(jnp.float32)
    rows, width = grad.shape
    mean = jnp.sum(grad * grad, axis=1, keepdims=True) * (1.0 / width)
    across = jnp.sum(
        jnp.where(iota((rows, rows), 0) == iota((rows, rows), 1), mean, 0.0), axis=0, keepdims=True
    )
    down = jnp.sum(
        jnp.where(iota((rows, rows), 0) == iota((rows, rows), 1), accum_ref[...], 0.0),
        axis=1,
        keepdims=True,
    )
    new_accum_ref[...] = accum_ref[...] + across
    new_table_ref[...] = table_ref[...] - learn_rate * grad / jnp.sqrt(down + mean)


def on_device(
    table, accum, item_weight, query_weight, packed_rows, block_counts, item_refs, query_refs
):
    bf16, f32, i32 = jnp.bfloat16, jnp.float32, jnp.int32
    shape = jax.ShapeDtypeStruct
    n_dp, n_table = lax.axis_size("dp"), lax.axis_size("table")
    chips = n_dp // CORES
    per, width = table.shape
    pairs = item_refs.shape[2]
    slots = CAP * n_dp
    base = slots * 3 // 4
    more = slots - base
    replica = lax.axis_index("dp")
    core = (replica % CORES).reshape(1).astype(i32)
    chip = (replica // CORES).reshape(1).astype(i32)
    along_y = [[y * CORES + c for y in range(chips)] for c in range(CORES)]
    along_parity = [
        [(2 * k + p) * CORES + c for k in range(chips // 2)] for p in range(2) for c in range(CORES)
    ]
    swap = [(r, r ^ 1) for r in range(n_dp)]
    beside = [
        (y * CORES + c, (y + (chips - 1 if c == 0 else 1)) % chips * CORES + c)
        for y in range(chips)
        for c in range(CORES)
    ]

    def over_y(x):
        return lax.all_to_all(
            x, "dp", split_axis=0, concat_axis=0, axis_index_groups=along_y, tiled=True
        )

    def over_table(x):
        parts = x.reshape(n_table, -1, x.shape[-1])
        return lax.all_to_all(parts, "table", split_axis=0, concat_axis=0, tiled=True).reshape(x.shape)

    near_rows = lax.all_to_all(
        jnp.broadcast_to(table.astype(bf16)[None], (chips // 2, per, width)),
        "dp",
        split_axis=0,
        concat_axis=0,
        axis_index_groups=along_parity,
        tiled=True,
    )
    items, queries = item_refs[0, 0].T, query_refs[0, 0].T
    requests, places, old_accum = call(
        functools.partial(request_body, base=base),
        (shape((n_table, slots + 8), i32), shape((n_table, slots), i32), shape((1, per), f32)),
        [SMEM] * 2 + [VMEM] * 5,
        [
            pltpu.VMEM((32, LANES), f32),
            pltpu.VMEM((n_dp * n_table // LANES, LANES), f32),
            pltpu.VMEM((LANES, LANES), f32),
        ],
    )(chip, core, packed_rows.reshape(1, -1), block_counts.reshape(1, -1), items, queries, accum.reshape(1, per))
    near_rows, requests = lax.optimization_barrier((near_rows, requests))
    next_rows = lax.ppermute(near_rows, "dp", beside)
    received = over_table(requests)
    received, near_rows, next_rows = lax.optimization_barrier((received, near_rows, next_rows))
    far_rows = lax.ppermute(jnp.concatenate([near_rows, next_rows]), "dp", swap)

    def pick_near(first, count, received):
        return call(
            functools.partial(pick_near_body, first=first, count=count, slots=slots),
            (shape((n_table * count, width), bf16), shape((LANES, LANES), i32), shape((1,), i32)),
            [VMEM] * 3,
            [pltpu.VMEM((LANES, LANES), f32)],
            out_specs=(VMEM, VMEM, SMEM),
        )(received, near_rows, next_rows)

    def pick_far(first, count, turned, near_got):
        return call(
            functools.partial(pick_far_body, first=first, count=count),
            shape((n_table * count, width), bf16),
            [VMEM] * 3,
        )(turned, far_rows, near_got)

    near_got, turned, over = pick_near(0, base, received)
    near_got, crowded, base_pos, more_pos, codes, more_codes, tower_weights = lax.optimization_barrier(
        (
            near_got,
            over[0] > 0,
            places[:, :base].reshape(1, -1),
            places[:, base:].reshape(1, -1),
            received[:, :base].reshape(1, -1),
            received[:, base:slots].reshape(1, -1),
            jnp.stack([item_weight, query_weight]),
        )
    )
    fetched = over_table(pick_far(0, base, turned, near_got))
    nothing = jnp.zeros((n_table * more, width), bf16)
    late, fetched = lax.optimization_barrier((received, fetched))
    more_fetched = lax.cond(
        crowded,
        lambda: over_table(pick_far(base, more, turned, pick_near(base, more, late)[0])),
        lambda: nothing,
    )
    pair_hits, more_hits, pool, spread = call(
        tower_body,
        (
            shape((2 * pairs, n_table * base), bf16),
            shape((2 * pairs, n_table * more), bf16),
            shape((2 * pairs, width), bf16),
            shape((chips, 2 * pairs, width), bf16),
        ),
        [VMEM] * 6 + [pl.BlockSpec(memory_space=pl.ANY), VMEM],
        [
            pltpu.VMEM((LANES, LANES), f32),
            pltpu.VMEM((2 * pairs, width), f32),
            pltpu.VMEM((n_table * more, width), bf16),
            pltpu.SemaphoreType.DMA,
        ],
    )(
        received,
        base_pos,
        more_pos,
        items,
        queries,
        fetched,
        more_fetched,
        tower_weights,
    )
    near = over_y(spread)
    far = lax.ppermute(near, "dp", swap)
    near_sums, normed, factor, turned_hits, more_turned_hits = call(
        near_body,
        (
            shape((chips, 1, pairs), f32),
            shape((2 * pairs, width), f32),
            shape((2 * pairs, LANES), f32),
            shape((n_table * base, 2 * pairs), bf16),
            shape((n_table * more, 2 * pairs), bf16),
        ),
        [VMEM] * 5,
    )(near, pool, tower_weights, pair_hits, more_hits)
    loss, grads, more_grads = call(
        loss_body,
        (
            shape((1, pairs), f32),
            shape((n_table * base, width), bf16),
            shape((n_table * more, width), bf16),
        ),
        [SMEM] + [VMEM] * 8,
        [pltpu.VMEM((chips, 1, 2 * pairs), f32), pltpu.VMEM((chips, pairs, 2 * pairs), f32)],
    )(chip, near, far, near_sums, normed, factor, tower_weights, turned_hits, more_turned_hits)
    returned = over_table(grads)
    more_returned = lax.cond(crowded, lambda: over_table(more_grads), lambda: nothing)

    def column(side, dtype):
        return call(
            functools.partial(column_body, side=side),
            shape((chips, per, width), dtype),
            [SMEM] + [VMEM] * 4,
        )(chip, codes, more_codes, returned, more_returned)

    other = lax.ppermute(column(1, bf16), "dp", swap)
    both = call(add_body, shape((chips, per, width), bf16), [VMEM] * 2)(column(0, f32), other)
    new_table, new_accum = call(
        adagrad_body, (shape((per, width), f32), shape((1, per), f32)), [VMEM] * 3
    )(over_y(both), table, old_accum)
    return (new_table, new_accum.reshape(per), loss.reshape(1, 1, pairs))


def solution(mesh):
    in_specs = (
        P(("dp", "table"), None),
        P(("dp", "table")),
        P(),
        P(),
        P("dp", "table", None),
        P("dp", "table", None),
        P("dp", "table", None, None),
        P("dp", "table", None, None),
    )
    out_specs = (P(("dp", "table"), None), P(("dp", "table")), P("dp", "table", None))
    return jax.shard_map(
        on_device, mesh=mesh, in_specs=in_specs, out_specs=out_specs, check_vma=False
    )
```

```python
import functools
import math

import jax
import jax.numpy as jnp
from jax import lax
from jax.experimental import pallas as pl
from jax.experimental.pallas import tpu as pltpu
from jax.sharding import PartitionSpec as P

CAP = 2
LANES = 128
CORES = 2

learn_rate = 0.3
epsilon = 1e-06
sharpness = 3.0

VMEM = pl.BlockSpec(memory_space=pltpu.VMEM)
SMEM = pl.BlockSpec(memory_space=pltpu.SMEM)

NT = (((1,), (1,)), ((), ()))


def iota(shape, axis):
    return lax.broadcasted_iota(jnp.int32, shape, axis)


def dot(a, b, dims=(((1,), (0,)), ((), ()))):
    return lax.dot_general(a, b, dims, preferred_element_type=jnp.float32)


def hits(a, b):
    return jnp.where(a == b, 1.0, 0.0)


def call(body, out_shape, in_specs, scratch=(), out_specs=None):
    return pl.pallas_call(
        body,
        out_shape=out_shape,
        in_specs=in_specs,
        out_specs=jax.tree.map(lambda _: VMEM, out_shape) if out_specs is None else out_specs,
        scratch_shapes=list(scratch),
        compiler_params=pltpu.CompilerParams(vmem_limit_bytes=12 * 1024 * 1024),
    )


def request_body(
    y_ref, core_ref, list_ref, counts_ref, item_refs, query_refs, accum_ref,
    req_ref, pos_ref, accum_out, looked, counts2d, square, *, base,
):
    length, owners = list_ref.shape[1], counts_ref.shape[1]
    rows = owners // LANES
    depth = looked.shape[0] // 2
    groups, slots = pos_ref.shape
    accum_out[...] = accum_ref[...]
    looked[...] = jnp.zeros_like(looked)
    for b in range(length // LANES):
        looked[b : b + 1, :] = list_ref[:, b * LANES : (b + 1) * LANES].astype(jnp.float32)
    for b in range(rows):
        counts2d[b : b + 1, :] = counts_ref[:, b * LANES : (b + 1) * LANES].astype(jnp.float32)
    down = iota((LANES, LANES), 0)
    block = iota((depth, LANES), 0)
    wanted = jnp.zeros((depth, LANES), jnp.float32)
    for refs_ref in (item_refs, query_refs):
        for l in range(refs_ref.shape[0]):
            ref = refs_ref[l : l + 1, :]
            high = hits(block, ref >> 7).astype(jnp.bfloat16)
            low = hits(down, ref & (LANES - 1)).astype(jnp.bfloat16)
            wanted = wanted + dot(high, low, NT)
    looked[depth:, :] = jnp.where(wanted > 0.5, 1.0, 0.0)
    looked_bf = looked[...].astype(jnp.bfloat16)

    counts = counts2d[...]
    counts_bf = counts.astype(jnp.bfloat16)
    before = hits(down < iota((LANES, LANES), 1), True).astype(jnp.bfloat16)
    within = dot(counts_bf, before)
    row_total = dot(counts_bf, jnp.ones((LANES, LANES), jnp.bfloat16))
    offsets = [jnp.zeros((1, LANES), jnp.float32)]
    for i in range(rows - 1):
        offsets.append(offsets[-1] + row_total[i : i + 1, :])
    starts = within + jnp.concatenate(offsets, axis=0)
    second = jnp.where(counts > 1.5, starts + 1.0, -1.0)
    positions = jnp.concatenate([starts, second], axis=0)
    pos_int = positions.astype(jnp.int32)
    entries = CAP * rows
    width = LANES // CORES
    owner_core = jnp.where(iota((1, LANES), 1) < width, 0, 1)
    side = jnp.where(owner_core == core_ref[0], 0.0, 1.0)
    parity = y_ref[0] % 2
    square[...] = jnp.zeros_like(square)
    square[entries : 2 * entries, :] = positions
    for r in range(entries):
        p = pos_int[r : r + 1, :]
        spread = dot(looked_bf, hits(down, p & (LANES - 1)).astype(jnp.bfloat16))
        here = block == (p >> 7)
        value = jnp.sum(jnp.where(here, spread[:depth], 0.0), axis=0, keepdims=True)
        used = jnp.sum(jnp.where(here, spread[depth:], 0.0), axis=0, keepdims=True)
        y = r % rows
        apart = jnp.where(parity == y % 2, 0, rows // 2).astype(jnp.float32)
        square[r : r + 1, :] = value + (side * rows + apart + y // 2) * LANES
        square[2 * entries + r : 2 * entries + r + 1, :] = used
    turned = square[...].T

    def column(n):
        part = slice(n * entries, (n + 1) * entries)
        return jnp.concatenate([turned[:width, part], turned[width:, part]], axis=1)

    codes, places, used = column(0), column(1), column(2)
    before = hits(iota((slots, slots), 0) < iota((slots, slots), 1), True).astype(jnp.bfloat16)
    rank = dot(used.astype(jnp.bfloat16), before)
    rank = jnp.where(used > 0.5, rank, -1.0).astype(jnp.int32)
    slot = iota((groups, slots), 1)
    packed_codes = jnp.full((groups, slots), -1.0, jnp.float32)
    packed_places = packed_codes
    for k in range(slots):
        here = slot == rank[:, k : k + 1]
        packed_codes = jnp.where(here, codes[:, k : k + 1], packed_codes)
        packed_places = jnp.where(here, places[:, k : k + 1], packed_places)
    over = jnp.max(rank, axis=1, keepdims=True)
    over = jnp.max(over, axis=0, keepdims=True)
    over = jnp.where(over >= base, 1, 0)
    pos_ref[...] = packed_places.astype(jnp.int32)
    req_ref[:, :slots] = packed_codes.astype(jnp.int32)
    req_ref[:, slots:] = jnp.broadcast_to(over, (groups, req_ref.shape[1] - slots))


def pick_rows(turned_ref, row_refs, out_ref, first, count, begin):
    groups = out_ref.shape[0] // count
    rows = jnp.concatenate([ref[...].reshape(-1, ref.shape[-1]) for ref in row_refs], axis=0)
    lane = iota((count, LANES), 1)
    step = 8
    for t in range(0, groups, step):
        hot = []
        for u in range(t, t + step):
            code = jnp.broadcast_to(turned_ref[first : first + count, u : u + 1], (count, LANES))
            hot.append(
                jnp.concatenate(
                    [hits(lane + (begin + b * LANES), code) for b in range(rows.shape[0] // LANES)],
                    axis=1,
                )
            )
        hot = jnp.concatenate(hot, axis=0).astype(jnp.bfloat16)
        yield pl.ds(t * count, step * count), dot(hot, rows)


def pick_near_body(recv_ref, near_ref, next_ref, out_ref, turned_ref, over_ref, square, *, first, count, slots):
    groups = recv_ref.shape[0]
    square[...] = jnp.zeros_like(square)
    square[:groups, : recv_ref.shape[1]] = recv_ref[...].astype(jnp.float32)
    turned_ref[...] = square[...].T.astype(jnp.int32)
    over_ref[0] = jnp.max(turned_ref[slots : slots + 1, :groups])
    for span, got in pick_rows(turned_ref, (near_ref, next_ref), out_ref, first, count, 0):
        out_ref[span, :] = got.astype(jnp.bfloat16)


def pick_far_body(turned_ref, far_ref, near_got, out_ref, *, first, count):
    begin = far_ref.shape[0] * far_ref.shape[1]
    for span, got in pick_rows(turned_ref, (far_ref,), out_ref, first, count, begin):
        out_ref[span, :] = (got + near_got[span, :].astype(jnp.float32)).astype(jnp.bfloat16)


def project(pool, weight):
    hidden = dot(pool, weight)
    factor = lax.rsqrt(jnp.mean(hidden * hidden, axis=1, keepdims=True) + epsilon)
    return hidden * factor, factor


def pair_weight(refs, pos):
    weight = hits(refs[:, 0:1], pos)
    for l in range(1, refs.shape[1]):
        weight = weight + hits(refs[:, l : l + 1], pos)
    return weight.astype(jnp.bfloat16)


def tower_body(
    recv_ref, pos_ref, more_pos_ref, item_refs, query_refs, fetched, more_fetched, weights,
    hits_ref, more_hits_ref, pool_ref, out_ref, square, pool_sum, more_rows, sem,
):
    pairs = item_refs.shape[1]
    square[...] = jnp.zeros_like(square)
    square[0 : item_refs.shape[0], :] = item_refs[...].astype(jnp.float32)
    square[8 : 8 + query_refs.shape[0], :] = query_refs[...].astype(jnp.float32)
    turned = square[...].T.astype(jnp.int32)
    item_columns = turned[:, 0 : item_refs.shape[0]]
    query_columns = turned[:, 8 : 8 + query_refs.shape[0]]
    slots = (pos_ref.shape[1] + more_pos_ref.shape[1]) // recv_ref.shape[0]
    crowded = jnp.max(recv_ref[:, slots : slots + 1]) > 0
    spans = [pl.ds(side * pairs, pairs) for side in range(2)]
    for span, refs in zip(spans, (item_columns, query_columns)):
        weight = pair_weight(refs, pos_ref[...])
        hits_ref[span, :] = weight
        pool_sum[span, :] = dot(weight, fetched[...])
    more_hits_ref[...] = jnp.zeros_like(more_hits_ref)

    @pl.when(crowded)
    def _():
        copy = pltpu.make_async_copy(more_fetched, more_rows, sem)
        copy.start()
        copy.wait()
        for span, refs in zip(spans, (item_columns, query_columns)):
            weight = pair_weight(refs, more_pos_ref[...])
            more_hits_ref[span, :] = weight
            pool_sum[span, :] = pool_sum[span, :] + dot(weight, more_rows[...])

    outs = []
    for side, span in enumerate(spans):
        pool = pool_sum[span, :].astype(jnp.bfloat16)
        pool_ref[span, :] = pool
        outs.append(project(pool, weights[side])[0].astype(jnp.bfloat16))
    for y in range(out_ref.shape[0]):
        out_ref[y, :pairs, :] = outs[0]
        out_ref[y, pairs:, :] = outs[1]


def scale_of(width):
    return sharpness * width ** (-0.5)


def exp_of(products, width):
    return jnp.exp2(products * (scale_of(width) * math.log2(math.e)))


def near_body(
    near, pool_ref, weights_ref, hits_ref, more_hits_ref,
    sums_ref, normed_ref, factor_ref, turned_ref, more_turned_ref,
):
    chips, both, width = near.shape
    pairs = both // 2
    step = 256
    for weights, out in ((hits_ref, turned_ref), (more_hits_ref, more_turned_ref)):
        for s in range(0, weights.shape[1], step):
            out[s : s + step, :] = weights[:, s : s + step].T
    for side in range(2):
        span = pl.ds(side * pairs, pairs)
        normed, factor = project(pool_ref[span, :], weights_ref[side])
        normed_ref[span, :] = normed
        factor_ref[span, :] = jnp.broadcast_to(factor, (pairs, LANES))
    for y in range(0, chips, 2):
        q = jnp.concatenate([near[y, pairs:, :], near[y + 1, pairs:, :]], axis=0)
        total = jnp.zeros((8, both), jnp.float32)
        for j in range(0, chips, 2):
            items = jnp.concatenate([near[j, :pairs, :], near[j + 1, :pairs, :]], axis=0)
            e = exp_of(dot(items, q, NT), width)
            total = total + jnp.sum(e.reshape(both // 8, 8, both), axis=0)
        total = jnp.sum(total, axis=0, keepdims=True)
        sums_ref[y] = total[:, :pairs]
        sums_ref[y + 1] = total[:, pairs:]


def loss_body(
    y_ref, near, far, near_sums, normed_ref, factor_ref, weights_ref, turned_ref, more_turned_ref,
    loss_ref, grads_ref, more_grads_ref, inverse, own_exp,
):
    chips, both, width = near.shape
    pairs = both // 2
    scale = scale_of(width)
    own = y_ref[0]

    def items(y):
        return jnp.concatenate([near[y, :pairs, :], far[y, :pairs, :]], axis=0)

    def queries(y):
        return jnp.concatenate([near[y, pairs:, :], far[y, pairs:, :]], axis=0)

    def denominators(h, carry):
        y = 2 * h
        q = jnp.concatenate([queries(y), queries(y + 1)], axis=0)
        far_q = jnp.concatenate([far[y, pairs:, :], far[y + 1, pairs:, :]], axis=0)
        total = jnp.zeros((8, 2 * both), jnp.float32)
        far_total = jnp.zeros((8, both), jnp.float32)
        for j in range(0, chips, 2):
            far_items = jnp.concatenate([far[j, :pairs, :], far[j + 1, :pairs, :]], axis=0)
            near_items = jnp.concatenate([near[j, :pairs, :], near[j + 1, :pairs, :]], axis=0)
            e = exp_of(dot(far_items, q, NT), width)
            total = total + jnp.sum(e.reshape(both // 8, 8, 2 * both), axis=0)
            e = exp_of(dot(near_items, far_q, NT), width)
            far_total = far_total + jnp.sum(e.reshape(both // 8, 8, both), axis=0)
        total = jnp.sum(total, axis=0, keepdims=True)
        far_total = jnp.sum(far_total, axis=0, keepdims=True)
        for u in range(2):
            inverse[y + u] = jnp.concatenate(
                [
                    total[:, u * both : u * both + pairs] + near_sums[y + u],
                    total[:, u * both + pairs : (u + 1) * both] + far_total[:, u * pairs : (u + 1) * pairs],
                ],
                axis=1,
            )
        return carry

    for h in range(chips // 2):
        denominators(h, 0)
    item_own, query_own = near[own, :pairs, :], near[own, pairs:, :]
    own_hits = iota((pairs, pairs), 0) == iota((pairs, pairs), 1)
    diagonal = jnp.sum(
        jnp.where(own_hits, dot(item_own, query_own, NT) * scale, 0.0), axis=0, keepdims=True
    )
    loss_ref[...] = jnp.log(inverse[own][:, :pairs]) - diagonal
    ones = hits(iota((pairs, both), 0), iota((pairs, both), 1))
    grad_item = jnp.zeros((pairs, width), jnp.float32)
    row_total = jnp.zeros((pairs, LANES), jnp.float32)
    for y in range(chips):
        q = queries(y)
        soft = exp_of(dot(item_own, q, NT), width) * (1.0 / inverse[y])
        soft = soft - jnp.where(own == y, ones, 0.0)
        grad_item = grad_item + dot(soft.astype(jnp.bfloat16), q)
        e = exp_of(dot(query_own, items(y), NT), width)
        own_exp[y] = e
        for b in range(both // LANES):
            row_total = row_total + e[:, b * LANES : (b + 1) * LANES]
    row_inverse = 1.0 / jnp.sum(row_total, axis=1, keepdims=True)
    grad_query = jnp.zeros((pairs, width), jnp.float32)
    for y in range(chips):
        soft = own_exp[y] * row_inverse - jnp.where(own == y, ones, 0.0)
        grad_query = grad_query + dot(soft.astype(jnp.bfloat16), items(y))
    backs = []
    for side, grad in enumerate((grad_item, grad_query)):
        span = pl.ds(side * pairs, pairs)
        grad = grad * scale
        normed, factor = normed_ref[span, :], factor_ref[span, 0:1]
        inner_mean = jnp.mean(grad * normed, axis=1, keepdims=True)
        grad_hidden = (factor * (grad - normed * inner_mean)).astype(jnp.bfloat16)
        backs.append(dot(grad_hidden, weights_ref[side], NT))
    back = jnp.concatenate(backs, axis=0).astype(jnp.bfloat16)
    for weights, out in ((turned_ref, grads_ref), (more_turned_ref, more_grads_ref)):
        out[...] = dot(weights[...], back).astype(jnp.bfloat16)


def column_body(y_ref, codes_ref, more_codes_ref, grads_ref, more_grads_ref, out_ref, *, side):
    chips, per = out_ref.shape[:2]
    parity = y_ref[0] % 2
    for n in range(0, chips, 2):
        begin = (side * chips + n) * per
        total = None
        for codes, grads in ((codes_ref, grads_ref), (more_codes_ref, more_grads_ref)):
            down = iota((2 * per, codes.shape[1]), 0)
            hot = hits(down, codes[...] - begin).astype(jnp.bfloat16)
            part = dot(hot, grads[...])
            total = part if total is None else total + part
        for u in range(2):
            half, k = divmod(n + u, chips // 2)
            owner_y = 2 * k + (parity if half == 0 else 1 - parity)
            out_ref[owner_y] = total[u * per : (u + 1) * per].astype(out_ref.dtype)


def add_body(a_ref, b_ref, out_ref):
    out_ref[...] = (a_ref[...] + b_ref[...].astype(jnp.float32)).astype(jnp.bfloat16)


def adagrad_body(parts_ref, table_ref, accum_ref, new_table_ref, new_accum_ref):
    grad = parts_ref[0].astype(jnp.float32)
    for y in range(1, parts_ref.shape[0]):
        grad = grad + parts_ref[y].astype(jnp.float32)
    rows, width = grad.shape
    mean = jnp.sum(grad * grad, axis=1, keepdims=True) * (1.0 / width)
    across = jnp.sum(
        jnp.where(iota((rows, rows), 0) == iota((rows, rows), 1), mean, 0.0), axis=0, keepdims=True
    )
    down = jnp.sum(
        jnp.where(iota((rows, rows), 0) == iota((rows, rows), 1), accum_ref[...], 0.0),
        axis=1,
        keepdims=True,
    )
    new_accum_ref[...] = accum_ref[...] + across
    new_table_ref[...] = table_ref[...] - learn_rate * grad / jnp.sqrt(down + mean)


def on_device(
    table, accum, item_weight, query_weight, packed_rows, block_counts, item_refs, query_refs
):
    bf16, f32, i32 = jnp.bfloat16, jnp.float32, jnp.int32
    shape = jax.ShapeDtypeStruct
    n_dp, n_table = lax.axis_size("dp"), lax.axis_size("table")
    chips = n_dp // CORES
    per, width = table.shape
    pairs = item_refs.shape[2]
    slots = CAP * n_dp
    base = slots * 3 // 4
    more = slots - base
    replica = lax.axis_index("dp")
    core = (replica % CORES).reshape(1).astype(i32)
    chip = (replica // CORES).reshape(1).astype(i32)
    along_y = [[y * CORES + c for y in range(chips)] for c in range(CORES)]
    along_parity = [
        [(2 * k + p) * CORES + c for k in range(chips // 2)] for p in range(2) for c in range(CORES)
    ]
    swap = [(r, r ^ 1) for r in range(n_dp)]
    beside = [
        (y * CORES + c, (y + (chips - 1 if c == 0 else 1)) % chips * CORES + c)
        for y in range(chips)
        for c in range(CORES)
    ]

    def over_y(x):
        return lax.all_to_all(
            x, "dp", split_axis=0, concat_axis=0, axis_index_groups=along_y, tiled=True
        )

    def over_table(x):
        parts = x.reshape(n_table, -1, x.shape[-1])
        return lax.all_to_all(parts, "table", split_axis=0, concat_axis=0, tiled=True).reshape(x.shape)

    near_rows = lax.all_to_all(
        jnp.broadcast_to(table.astype(bf16)[None], (chips // 2, per, width)),
        "dp",
        split_axis=0,
        concat_axis=0,
        axis_index_groups=along_parity,
        tiled=True,
    )
    items, queries = item_refs[0, 0].T, query_refs[0, 0].T
    requests, places, old_accum = call(
        functools.partial(request_body, base=base),
        (shape((n_table, slots + 8), i32), shape((n_table, slots), i32), shape((1, per), f32)),
        [SMEM] * 2 + [VMEM] * 5,
        [
            pltpu.VMEM((32, LANES), f32),
            pltpu.VMEM((n_dp * n_table // LANES, LANES), f32),
            pltpu.VMEM((LANES, LANES), f32),
        ],
    )(chip, core, packed_rows.reshape(1, -1), block_counts.reshape(1, -1), items, queries, accum.reshape(1, per))
    near_rows, requests = lax.optimization_barrier((near_rows, requests))
    next_rows = lax.ppermute(near_rows, "dp", beside)
    received = over_table(requests)
    received, near_rows, next_rows = lax.optimization_barrier((received, near_rows, next_rows))
    far_rows = lax.ppermute(jnp.concatenate([near_rows, next_rows]), "dp", swap)

    def pick_near(first, count, received):
        return call(
            functools.partial(pick_near_body, first=first, count=count, slots=slots),
            (shape((n_table * count, width), bf16), shape((LANES, LANES), i32), shape((1,), i32)),
            [VMEM] * 3,
            [pltpu.VMEM((LANES, LANES), f32)],
            out_specs=(VMEM, VMEM, SMEM),
        )(received, near_rows, next_rows)

    def pick_far(first, count, turned, near_got):
        return call(
            functools.partial(pick_far_body, first=first, count=count),
            shape((n_table * count, width), bf16),
            [VMEM] * 3,
        )(turned, far_rows, near_got)

    near_got, turned, over = pick_near(0, base, received)
    near_got, codes, more_codes = lax.optimization_barrier(
        (
            near_got,
            received[:, :base].reshape(1, -1),
            received[:, base:slots].reshape(1, -1),
        )
    )
    crowded = over[0] > 0
    base_pos = places[:, :base].reshape(1, -1)
    more_pos = places[:, base:].reshape(1, -1)
    tower_weights = jnp.stack([item_weight, query_weight])
    fetched = over_table(pick_far(0, base, turned, near_got))
    nothing = jnp.zeros((n_table * more, width), bf16)
    late, fetched = lax.optimization_barrier((received, fetched))
    more_fetched = lax.cond(
        crowded,
        lambda: over_table(pick_far(base, more, turned, pick_near(base, more, late)[0])),
        lambda: nothing,
    )
    pair_hits, more_hits, pool, spread = call(
        tower_body,
        (
            shape((2 * pairs, n_table * base), bf16),
            shape((2 * pairs, n_table * more), bf16),
            shape((2 * pairs, width), bf16),
            shape((chips, 2 * pairs, width), bf16),
        ),
        [VMEM] * 6 + [pl.BlockSpec(memory_space=pl.ANY), VMEM],
        [
            pltpu.VMEM((LANES, LANES), f32),
            pltpu.VMEM((2 * pairs, width), f32),
            pltpu.VMEM((n_table * more, width), bf16),
            pltpu.SemaphoreType.DMA,
        ],
    )(
        received,
        base_pos,
        more_pos,
        items,
        queries,
        fetched,
        more_fetched,
        tower_weights,
    )
    near = over_y(spread)
    far = lax.ppermute(near, "dp", swap)
    near_sums, normed, factor, turned_hits, more_turned_hits = call(
        near_body,
        (
            shape((chips, 1, pairs), f32),
            shape((2 * pairs, width), f32),
            shape((2 * pairs, LANES), f32),
            shape((n_table * base, 2 * pairs), bf16),
            shape((n_table * more, 2 * pairs), bf16),
        ),
        [VMEM] * 5,
    )(near, pool, tower_weights, pair_hits, more_hits)
    loss, grads, more_grads = call(
        loss_body,
        (
            shape((1, pairs), f32),
            shape((n_table * base, width), bf16),
            shape((n_table * more, width), bf16),
        ),
        [SMEM] + [VMEM] * 8,
        [pltpu.VMEM((chips, 1, 2 * pairs), f32), pltpu.VMEM((chips, pairs, 2 * pairs), f32)],
    )(chip, near, far, near_sums, normed, factor, tower_weights, turned_hits, more_turned_hits)
    returned = over_table(grads)
    more_returned = lax.cond(crowded, lambda: over_table(more_grads), lambda: nothing)

    def column(side, dtype):
        return call(
            functools.partial(column_body, side=side),
            shape((chips, per, width), dtype),
            [SMEM] + [VMEM] * 4,
        )(chip, codes, more_codes, returned, more_returned)

    other = lax.ppermute(column(1, bf16), "dp", swap)
    both = call(add_body, shape((chips, per, width), bf16), [VMEM] * 2)(column(0, f32), other)
    new_table, new_accum = call(
        adagrad_body, (shape((per, width), f32), shape((1, per), f32)), [VMEM] * 3
    )(over_y(both), table, old_accum)
    return (new_table, new_accum.reshape(per), loss.reshape(1, 1, pairs))


def solution(mesh):
    in_specs = (
        P(("dp", "table"), None),
        P(("dp", "table")),
        P(),
        P(),
        P("dp", "table", None),
        P("dp", "table", None),
        P("dp", "table", None, None),
        P("dp", "table", None, None),
    )
    out_specs = (P(("dp", "table"), None), P(("dp", "table")), P("dp", "table", None))
    return jax.shard_map(
        on_device, mesh=mesh, in_specs=in_specs, out_specs=out_specs, check_vma=False
    )
```
